128 devices in a mesh: batch: 8 (over z, core), proto: 16 (over y, x).
Axes of the slice: x: 4, y: 4, z: 4, core: 2. Of those that a mesh axis runs over, the one named last changes fastest.
Arguments:
- student_patches: bfloat16 [256, 256, 256], P(('batch', 'proto')), may hold values from -4 to 4
- teacher_patches: bfloat16 [256, 256, 256], P(('batch', 'proto')), may hold values from -8 to 8
- mask_positions: int32 [256, 32], P(('batch', 'proto')), may hold values from 0 to 255, as said below
- token_weight: bfloat16 [256, 32], P(('batch', 'proto')), may hold values from 0.5 to 8
- student_weight: bfloat16 [131072, 256], P('proto'), may hold values from -4 to 4
- teacher_weight: bfloat16 [131072, 256], P('proto'), may hold values from -4 to 4
Outputs:
- loss: float32 [], replicated
- feature_grads: float32 [256, 32, 256], P(('batch', 'proto'))
- weight_grads: float32 [131072, 256], P(('proto', 'batch'))
The draws below stay inside these ranges and needn't reach their ends.
Inputs may be any that keep to these rules, and one draw needn't show every extreme that they name: `mask_positions`: each row holds 32 different patch indices.
All inputs are finite; a program needn't handle non-finite values.
Results may differ from the reference program's by a relative error of at most 0.0039.
Values may be sent and summed in bfloat16 or wider, within the bound.
No kernel may reach another device: no remote copies, remote signals or barrier semaphores. Data moves between devices by JAX's collectives and lax.ppermute only.
A program may use at most 256 MiB of HBM per device.

```python
from functools import partial
import jax
import jax.numpy as jnp
from jax import lax

D = 256
PATCHES = 256
PROTO_DEV = 8192
MASKED = 32
SWEEPS = 3
K = 131072
IMAGES = 256
TOKENS = 8192
N_PROTO = 16


concept_count = 64


def shared_concepts(key):
    concept_key, image_key, proto_key = jax.random.split(key, 3)
    concepts = jax.random.normal(concept_key, (concept_count, D), jnp.float32) * D ** (-0.5)
    image_concept = jax.random.randint(image_key, (IMAGES,), 0, concept_count)
    proto_concept = jax.random.randint(proto_key, (K,), 0, concept_count)
    return (concepts, image_concept, proto_concept)


def draw_teacher_patches(key, part):
    concepts, image_concept, proto_concept = shared_concepts(key)
    key = jax.random.fold_in(key, 11)
    noise_key, align_key = jax.random.split(key, 2)
    noise = jax.random.normal(noise_key, (IMAGES, PATCHES, D), jnp.float32) * D ** (-0.5)
    align = jax.random.uniform(align_key, (IMAGES, PATCHES, 1), jnp.float32, 0.25, 0.9)
    scale = 2.0
    centre = jnp.take(concepts, image_concept, axis=0)[:, None, :]
    values = scale * (align * centre + jnp.sqrt(1.0 - align * align) * noise)
    return jnp.clip(values, -8.0, 8.0).astype(jnp.bfloat16)


def draw_teacher_weight(key, part):
    concepts, image_concept, proto_concept = shared_concepts(key)
    key = jax.random.fold_in(key, 47)
    noise_key, align_key = jax.random.split(key, 2)
    noise = jax.random.normal(noise_key, (K, D), jnp.float32) * D ** (-0.5)
    align = jax.random.uniform(align_key, (K, 1), jnp.float32, 0.15, 0.9)
    centre = jnp.take(concepts, proto_concept, axis=0)
    values = align * centre + jnp.sqrt(1.0 - align * align) * noise
    return jnp.clip(values, -4.0, 4.0).astype(jnp.bfloat16)


def draw_student_patches(key, part):
    concepts, image_concept, proto_concept = shared_concepts(key)
    key = jax.random.fold_in(key, 59)
    noise_key, align_key = jax.random.split(key, 2)
    noise = jax.random.normal(noise_key, (IMAGES, PATCHES, D), jnp.float32) * D ** (-0.5)
    align = jax.random.uniform(align_key, (IMAGES, PATCHES, 1), jnp.float32, 0.55, 0.9)
    centre = jnp.take(concepts, image_concept, axis=0)[:, None, :]
    values = align * centre + jnp.sqrt(1.0 - align * align) * noise
    return jnp.clip(values, -4.0, 4.0).astype(jnp.bfloat16)


def draw_student_weight(key, part):
    concepts, image_concept, proto_concept = shared_concepts(key)
    key = jax.random.fold_in(key, 71)
    noise_key, align_key = jax.random.split(key, 2)
    place = (jnp.arange(K, dtype=jnp.float32) / K)[:, None]
    noise = jax.random.normal(noise_key, (K, D), jnp.float32) * D ** (-0.5)
    align = 0.8 * place * jax.random.uniform(align_key, (K, 1), jnp.float32, 0.75, 1.0)
    centre = jnp.take(concepts, proto_concept, axis=0)
    values = align * centre + jnp.sqrt(1.0 - align * align) * noise
    return jnp.clip(values, -4.0, 4.0).astype(jnp.bfloat16)


def draw_mask_positions(key, part):
    key = jax.random.fold_in(key, 23)
    row_keys = jax.random.split(key, IMAGES)
    chosen = jax.vmap(lambda row_key: jax.random.permutation(row_key, PATCHES)[:MASKED])(row_keys)
    return chosen.astype(jnp.int32)


def draw_token_weight(key, part):
    key = jax.random.fold_in(key, 37)
    ranks = (jnp.arange(IMAGES, dtype=jnp.float32) / IMAGES)[:, None]
    logs = jax.random.uniform(key, (IMAGES, MASKED), jnp.float32, -0.693, 0.693)
    values = jnp.exp(logs) * (1.0 + 2.0 * ranks)
    return jnp.clip(values, 0.5, 8.0).astype(jnp.bfloat16)


def setup_inputs(seed: int = 0) -> dict:
    key_of = jax.random.split(jax.random.key(seed), 7)
    return {
        "student_patches": draw_student_patches(jax.random.fold_in(key_of[6], 71), 0),
        "teacher_patches": draw_teacher_patches(jax.random.fold_in(key_of[6], 71), 0),
        "mask_positions": draw_mask_positions(jax.random.fold_in(key_of[6], 71), 0),
        "token_weight": draw_token_weight(jax.random.fold_in(key_of[6], 71), 0),
        "student_weight": draw_student_weight(jax.random.fold_in(key_of[6], 71), 0),
        "teacher_weight": draw_teacher_weight(jax.random.fold_in(key_of[6], 71), 0),
    }


teacher_temp = 0.07
student_temp = 0.1
epsilon = 1e-06

def normalize_rows(values):
    scale = lax.rsqrt(lax.optimization_barrier(jnp.sum(values * values, axis=-1, keepdims=True)) + epsilon)
    return (values * scale, scale)

def normalize_back(unit, scale, grad):
    return scale * (grad - unit * lax.optimization_barrier(jnp.sum(unit * grad, axis=-1, keepdims=True)))

def teacher_block(teacher_unit, block):
    protos = normalize_rows(block.astype(jnp.float32))[0].astype(jnp.bfloat16)
    scores = jnp.dot(teacher_unit, protos.T, preferred_element_type=jnp.float32)
    return jnp.exp(scores / teacher_temp)

def sweep_block(teacher_unit, token_scale, column_mass, block):
    expo = teacher_block(teacher_unit, block)
    proto_scale = 1.0 / jnp.dot(token_scale, expo, precision=lax.Precision.HIGHEST)
    column_mass = column_mass + jnp.dot(expo, proto_scale, precision=lax.Precision.HIGHEST)
    return (column_mass, proto_scale)

def reference(student_patches, teacher_patches, mask_positions, token_weight, student_weight, teacher_weight):
    index = mask_positions.astype(jnp.int32)[:, :, None]
    student_rows = jnp.take_along_axis(student_patches, index, axis=1).reshape(TOKENS, D)
    teacher_rows = jnp.take_along_axis(teacher_patches, index, axis=1).reshape(TOKENS, D)
    student_float, student_scale = normalize_rows(student_rows.astype(jnp.float32))
    student_unit = student_float.astype(jnp.bfloat16)
    teacher_unit = normalize_rows(teacher_rows.astype(jnp.float32))[0].astype(jnp.bfloat16)
    weights = token_weight.reshape(TOKENS).astype(jnp.float32)
    student_blocks = student_weight.reshape(N_PROTO, PROTO_DEV, D)
    teacher_blocks = teacher_weight.reshape(N_PROTO, PROTO_DEV, D)
    token_scale = jnp.ones((TOKENS,), jnp.float32)
    proto_scale = jnp.ones((N_PROTO, PROTO_DEV), jnp.float32)
    for sweep in range(SWEEPS):
        column_mass, proto_scale = lax.scan(partial(sweep_block, teacher_unit, token_scale), jnp.zeros((TOKENS,), jnp.float32), teacher_blocks)
        token_scale = 1.0 / column_mass

    def total_step(totals, block):
        protos = normalize_rows(block.astype(jnp.float32))[0].astype(jnp.bfloat16)
        cosines = jnp.dot(student_unit, protos.T, preferred_element_type=jnp.float32)
        return (totals + lax.optimization_barrier(jnp.sum(jnp.exp(cosines / student_temp), axis=1)), None)
    totals, unused = lax.scan(total_step, jnp.zeros((TOKENS,), jnp.float32), student_blocks)
    log_total = jnp.log(totals)

    def final_step(carry, items):
        cross, unit_grads = carry
        student_block, teacher_blk, scale_block = items
        proto_float, proto_norm = normalize_rows(student_block.astype(jnp.float32))
        protos = proto_float.astype(jnp.bfloat16)
        targets = teacher_block(teacher_unit, teacher_blk) * scale_block[None, :] * token_scale[:, None]
        cosines = jnp.dot(student_unit, protos.T, preferred_element_type=jnp.float32)
        log_prob = cosines / student_temp - log_total[:, None]
        cross = cross - lax.optimization_barrier(jnp.sum(targets * log_prob, axis=1))
        probs = jnp.exp(cosines / student_temp) / totals[:, None]
        logit_grads = (weights[:, None] * (probs - targets) / student_temp).astype(jnp.bfloat16)
        unit_grads = unit_grads + jnp.dot(logit_grads, protos, preferred_element_type=jnp.float32)
        proto_grads = jnp.dot(logit_grads.T, student_unit, preferred_element_type=jnp.float32)
        return ((cross, unit_grads), normalize_back(proto_float, proto_norm, proto_grads))
    start = (jnp.zeros((TOKENS,), jnp.float32), jnp.zeros((TOKENS, D), jnp.float32))
    (cross, unit_grads), weight_blocks = lax.scan(final_step, start, (student_blocks, teacher_blocks, proto_scale))
    loss = jnp.sum(weights * cross) / TOKENS
    feature_grads = normalize_back(student_float, student_scale, unit_grads).reshape(IMAGES, MASKED, D)
    weight_grads = weight_blocks.reshape(K, D)
    return (loss, feature_grads, weight_grads)
```

```python
import jax
import jax.numpy as jnp
from jax import lax
from jax.experimental import pallas as pl
from jax.experimental.pallas import tpu as pltpu
from jax.sharding import Mesh, PartitionSpec as P

teacher_temp = 0.07
student_temp = 0.1
epsilon = 1e-06
LOG2E = 1.4426950408889634
SWEEPS = 3
TOKENS = 8192
T, K, D = 2048, 4096, 256
BLOCK = 512
LANES = 128
f32, bf16 = jnp.float32, jnp.bfloat16
SAME_TOKENS = ("x", "y", "zh")
VMEM = pl.BlockSpec(memory_space=pltpu.VMEM)
SMEM = pl.BlockSpec(memory_space=pltpu.SMEM)


def nt(left, right):
    return lax.dot_general(left, right, (((1,), (1,)), ((), ())), preferred_element_type=f32)


def nn(left, right):
    return lax.dot_general(left, right, (((1,), (0,)), ((), ())), preferred_element_type=f32)


def normalize_rows(values):
    scale = lax.rsqrt(jnp.sum(values * values, axis=-1, keepdims=True) + epsilon)
    return values * scale, scale


def three_rows(row):
    high = row.astype(bf16).astype(f32)
    rest = row - high
    middle = rest.astype(bf16).astype(f32)
    low = rest - middle
    index = lax.broadcasted_iota(jnp.int32, (16, row.shape[1]), 0)
    picked = jnp.where(index == 0, high, jnp.where(index == 1, middle, jnp.where(index == 2, low, 0.0)))
    return picked.astype(bf16)


def as_row(packed):
    return jnp.concatenate([packed[j : j + 1, :] for j in range(packed.shape[0])], axis=1)


def store_packed(ref, start, row):
    for j in range(row.shape[1] // LANES):
        ref[start + j : start + j + 1, :] = row[:, j * LANES : (j + 1) * LANES]


def call(kernel, outs, *args, scratch=(), limit=20, name=None):
    shapes, specs, operands = [], [], []
    for shape, dtype, resident in outs:
        shapes.append(pltpu.VMEM(shape, dtype) if resident else jax.ShapeDtypeStruct(shape, dtype))
    for arg in args:
        if arg.dtype == jnp.int32:
            specs.append(SMEM)
        else:
            specs.append(VMEM)
            if arg.shape == (K, T):
                arg = pltpu.with_memory_space_constraint(arg, pltpu.VMEM)
        operands.append(arg)
    return pl.pallas_call(
        kernel,
        out_shape=shapes,
        in_specs=specs,
        out_specs=[VMEM] * len(shapes),
        scratch_shapes=list(scratch),
        compiler_params=pltpu.CompilerParams(vmem_limit_bytes=limit << 20),
        name=name,
    )(*operands)


def lane_sums(values):
    part = values[:, 0:LANES]
    for j in range(1, values.shape[1] // LANES):
        part = part + values[:, j * LANES : (j + 1) * LANES]
    return jnp.sum(jnp.transpose(part), axis=0, keepdims=True)


def teacher_kernel(rows_ref, weight_ref, exp_ref, mass_ref):
    rows = rows_ref[...]
    for b in range(K // BLOCK):
        here = slice(b * BLOCK, (b + 1) * BLOCK)
        protos = normalize_rows(weight_ref[here, :].astype(f32))[0].astype(bf16)
        values = jnp.exp2(nt(protos, rows) * (LOG2E / teacher_temp))
        exp_ref[here, :] = values.astype(bf16)
        store_packed(mass_ref, b * BLOCK // LANES, lane_sums(values))


def student_kernel(rows_ref, weight_ref, exp_ref, total_ref, protos_t_ref, rows_t_ref):
    rows = rows_ref[...]
    rows_t_ref[...] = jnp.transpose(rows.astype(f32)).astype(bf16)
    total = jnp.zeros((8, T), f32)
    for b in range(K // BLOCK):
        here = slice(b * BLOCK, (b + 1) * BLOCK)
        protos = normalize_rows(weight_ref[here, :].astype(f32))[0].astype(bf16)
        protos_t_ref[:, here] = jnp.transpose(protos.astype(f32)).astype(bf16)
        values = jnp.exp2(nt(protos, rows) * (LOG2E / student_temp))
        exp_ref[here, :] = values.astype(bf16)
        total = total + jnp.sum(values.reshape(BLOCK // 8, 8, T), axis=0)
    store_packed(total_ref, 0, jnp.sum(total, axis=0, keepdims=True))


def proto_scale_of(own_ref, core_ref, z_ref, both_ref):
    return 1.0 / ((own_ref[...] + core_ref[...]) + (z_ref[...] + both_ref[...]))


def token_mass_kernel(own_ref, core_ref, z_ref, both_ref, exp_ref, mass_ref):
    scale = three_rows(as_row(proto_scale_of(own_ref, core_ref, z_ref, both_ref)))
    total = jnp.zeros((16, T), f32)
    for b in range(K // BLOCK):
        here = slice(b * BLOCK, (b + 1) * BLOCK)
        total = total + nn(scale[:, here], exp_ref[here, :])
    store_packed(mass_ref, 0, jnp.sum(total, axis=0, keepdims=True))


def last_token_mass_kernel(
    own_ref, core_ref, z_ref, both_ref, exp_ref, protos_t_ref, rows_t_ref,
    mass_ref, scale_ref, grads_ref, left_ref
):
    packed = proto_scale_of(own_ref, core_ref, z_ref, both_ref)
    scale_ref[...] = packed
    scale = as_row(packed)
    left_ref[0:D, :] = (protos_t_ref[...].astype(f32) * scale).astype(bf16)
    left_ref[D : D + 16, :] = three_rows(scale)
    for j in range(T // BLOCK):
        here = slice(j * BLOCK, (j + 1) * BLOCK)
        both = nn(left_ref[...], exp_ref[:, here])
        grads = both[0:D]
        grads_ref[:, here] = grads
        store_packed(mass_ref, j * BLOCK // LANES, jnp.sum(both[D:], axis=0, keepdims=True))
        cross = jnp.sum(grads * rows_t_ref[:, here].astype(f32), axis=0, keepdims=True)
        store_packed(mass_ref, (T + j * BLOCK) // LANES, cross)


def column_mass(scale, exp_ref, mass_ref):
    for b in range(K // BLOCK):
        part = jnp.zeros((BLOCK, LANES), f32)
        for j in range(T // LANES):
            lanes = slice(j * LANES, (j + 1) * LANES)
            part = part + exp_ref[b * BLOCK : (b + 1) * BLOCK, lanes].astype(f32) * scale[:, lanes]
        row = jnp.sum(jnp.transpose(part), axis=0, keepdims=True)
        store_packed(mass_ref, b * BLOCK // LANES, row)


def proto_mass_kernel(parts_ref, exp_ref, mass_ref):
    column_mass(1.0 / as_row(jnp.sum(parts_ref[...], axis=0)), exp_ref, mass_ref)


def first_proto_mass_kernel(parts_ref, exp_ref, mass_ref, total_ref, weight_ref):
    parts = jnp.sum(parts_ref[...], axis=0)
    total_ref[...] = parts[16:32]
    weight_ref[...] = parts[32:48]
    column_mass(1.0 / as_row(parts[0:16]), exp_ref, mass_ref)


def student_unit_kernel(protos_t_ref, exp_ref, out_ref):
    for j in range(T // BLOCK):
        here = slice(j * BLOCK, (j + 1) * BLOCK)
        out_ref[:, here] = nn(protos_t_ref[...], exp_ref[:, here])


def student_proto_kernel(rows_t_ref, total_ref, weight_ref, exp_ref, out_ref):
    scale = as_row(weight_ref[...] / (student_temp * total_ref[...]))
    right = (rows_t_ref[...].astype(f32) * scale).astype(bf16)
    for b in range(K // BLOCK):
        here = slice(b * BLOCK, (b + 1) * BLOCK)
        out_ref[here, :] = nt(exp_ref[here, :], right)


def combine_kernel(
    place_ref, parts_ref, total_ref, weight_ref, student_ref, teacher_ref,
    loss_ref, scale_ref, keep_ref, one_ref, two_ref, three_ref, rows_ref
):
    parts = jnp.sum(parts_ref[...], axis=0)
    token_scale = 1.0 / parts[0:16]
    total, weight = total_ref[...], weight_ref[...]
    cross = jnp.log(total) - token_scale * parts[16:32] / student_temp
    loss_ref[...] = jnp.full((8, LANES), jnp.sum(weight * cross) / TOKENS, f32)
    teacher_scale = weight * token_scale / student_temp
    scale_ref[...] = teacher_scale
    rows_ref[0:1, :] = as_row(weight / (student_temp * total))
    rows_ref[8:9, :] = as_row(teacher_scale)
    for step, ref in enumerate((keep_ref, one_ref, two_ref, three_ref)):
        block = lax.rem(place_ref[4] + step, 4)
        here = pl.ds(pl.multiple_of(block * 512, 512), 512)
        grads = student_ref[:, here] * rows_ref[0:1, here] - teacher_ref[:, here] * rows_ref[8:9, here]
        ref[...] = jnp.transpose(grads).astype(ref.dtype)


def fold_x_kernel(place_ref, own_ref, a_ref, b_ref, c_ref, keep_ref, one_ref, two_ref, three_ref):
    for step, ref in enumerate((keep_ref, one_ref, two_ref, three_ref)):
        block = lax.rem(place_ref[3] + step, 4)
        here = pl.ds(pl.multiple_of(block * 128, 128), 128)
        total = own_ref[here, :] + a_ref[here, :].astype(f32) + b_ref[here, :].astype(f32)
        ref[...] = (total + c_ref[here, :].astype(f32)).astype(ref.dtype)


def fold_y_kernel(place_ref, own_ref, a_ref, b_ref, c_ref, keep_ref, send_ref):
    for step, ref in enumerate((keep_ref, send_ref)):
        block = lax.rem(place_ref[0] + step, 2)
        here = pl.ds(pl.multiple_of(block * 64, 64), 64)
        total = own_ref[here, :] + a_ref[here, :].astype(f32) + b_ref[here, :].astype(f32)
        ref[...] = (total + c_ref[here, :].astype(f32)).astype(ref.dtype)


def proto_kernel(core_flip, place_ref, rows_t_ref, teacher_scale_ref, scale_ref, exp_ref, student_ref, near_ref, far_ref):
    right = (rows_t_ref[...].astype(f32) * as_row(teacher_scale_ref[...])).astype(bf16)
    core = place_ref[2] if core_flip == 0 else 1 - place_ref[2]
    for z, ref in ((1 - place_ref[1], far_ref), (place_ref[1], near_ref)):
        chunk = z * 2 + core
        for b in range(2):
            start = pl.multiple_of(chunk * 1024 + b * 512, 512)
            product = nt(exp_ref[pl.ds(start, 512), :], right)
            student = student_ref[pl.ds(start, 512), :]
            for j in range(4):
                row = scale_ref[pl.ds(chunk * 8 + b * 4 + j, 1), :]
                column = jnp.transpose(jnp.broadcast_to(row, (LANES, LANES)))
                column = jnp.concatenate([column, column], axis=1)
                here = slice(j * LANES, (j + 1) * LANES)
                value = student[here] - product[here] * column
                ref[b * 512 + j * LANES : b * 512 + (j + 1) * LANES, :] = value.astype(ref.dtype)


def normalize_back(unit, scale, grad):
    return scale * (grad - unit * jnp.sum(unit * grad, axis=-1, keepdims=True))


def weight_grads_kernel(place_ref, weight_ref, own_ref, core_ref, far_ref, out_ref):
    grads = own_ref[...] + core_ref[...].astype(f32) + far_ref[...].astype(f32)
    unit, scale = normalize_rows(weight_ref[...].astype(f32))
    out_ref[...] = normalize_back(unit, scale, grads)


def feature_grads_kernel(rows_ref, own_ref, far_ref, out_ref):
    unit, scale = normalize_rows(rows_ref[...].astype(f32))
    out_ref[...] = normalize_back(unit, scale, own_ref[...] + far_ref[...].astype(f32))


def shift(values, axis, step):
    return lax.ppermute(values, axis, [(i, (i + step) % 4) for i in range(4)])


def flip(values, axis):
    return lax.ppermute(values, axis, [(0, 1), (1, 0)])


def flip_both(values):
    return lax.ppermute(values, ("zl", "c"), [(i, 3 - i) for i in range(4)])


def over_token_groups(values):
    return values, flip(values, "c"), flip(values, "zl"), flip_both(values)


def over_proto_groups(values):
    copies = jnp.broadcast_to(values[None], (32,) + values.shape)
    return lax.all_to_all(copies, SAME_TOKENS, 0, 0, tiled=True)


def gather_rows(rows):
    copies = jnp.broadcast_to(rows[None], (32,) + rows.shape)
    return lax.all_to_all(copies, SAME_TOKENS, 0, 0, tiled=True).reshape(T, D)


def local(student_patches, teacher_patches, mask_positions, token_weight, student_weight, teacher_weight):
    zh, zl, c, y, x = (lax.axis_index(name) for name in ("zh", "zl", "c", "y", "x"))
    place = jnp.stack([zh, zl, c, y, x]).astype(jnp.int32)
    index = mask_positions[:, :, None]
    teacher_rows = jnp.take_along_axis(teacher_patches, index, axis=1).reshape(64, D)
    student_rows = jnp.take_along_axis(student_patches, index, axis=1).reshape(64, D)
    teacher_unit = normalize_rows(teacher_rows.astype(f32))[0].astype(bf16)
    student_unit = normalize_rows(student_rows.astype(f32))[0].astype(bf16)
    teacher_all = gather_rows(teacher_unit)
    student_all = gather_rows(student_unit)
    weight_here = lax.dynamic_update_slice(
        jnp.zeros((T,), f32), token_weight.reshape(64).astype(f32), (((x * 4 + y) * 2 + zh) * 64,)
    ).reshape(16, LANES)
    teacher_half = lax.dynamic_slice_in_dim(teacher_weight, zh * K, K, 0)
    student_half = lax.dynamic_slice_in_dim(student_weight, zh * K, K, 0)

    teacher_exp, mass = call(
        teacher_kernel, [((K, T), bf16, True), ((32, LANES), f32, False)], teacher_all, teacher_half,
        name="teacher_exp",
    )
    masses = over_token_groups(mass)
    student_exp, total, protos_t, rows_t = call(
        student_kernel,
        [((K, T), bf16, True), ((16, LANES), f32, False), ((D, K), bf16, False), ((D, T), bf16, False)],
        student_all, student_half, name="student_exp",
    )
    token_mass = [((16, LANES), f32, False)]
    proto_mass = [((32, LANES), f32, False)]
    (mass,) = call(token_mass_kernel, token_mass, *masses, teacher_exp, name="token_mass")
    parts = over_proto_groups(jnp.concatenate([mass, total, weight_here], axis=0))
    mass, total, weight = call(
        first_proto_mass_kernel, proto_mass + token_mass * 2, parts, teacher_exp, name="proto_mass"
    )
    masses = over_token_groups(mass)
    (student_part,) = call(
        student_unit_kernel, [((D, T), f32, False)], protos_t, student_exp, name="student_unit_grads"
    )
    (mass,) = call(token_mass_kernel, token_mass, *masses, teacher_exp, name="token_mass")
    parts = over_proto_groups(mass)
    (mass,) = call(proto_mass_kernel, proto_mass, parts, teacher_exp, name="proto_mass")
    masses = over_token_groups(mass)
    (student_proto,) = call(
        student_proto_kernel, [((K, D), f32, False)], rows_t, total, weight, student_exp,
        name="student_proto_grads",
    )
    mass, proto_scale, teacher_part = call(
        last_token_mass_kernel,
        [((32, LANES), f32, False), ((32, LANES), f32, False), ((D, T), f32, False)],
        *masses, teacher_exp, protos_t, rows_t,
        scratch=[pltpu.VMEM((D + 16, K), bf16)], name="last_token_mass",
    )
    parts = over_proto_groups(mass)
    loss, teacher_scale, own, one, two, three = call(
        combine_kernel,
        [((8, LANES), f32, False), ((16, LANES), f32, False), ((512, D), f32, False)]
        + [((512, D), bf16, False)] * 3,
        place, parts, total, weight, student_part, teacher_part,
        scratch=[pltpu.VMEM((16, T), f32)], name="combine",
    )
    one, two, three = shift(one, "x", 1), shift(two, "x", 2), shift(three, "x", 3)
    send_near, send_far = call(
        lambda *refs: proto_kernel(1, *refs),
        [((1024, D), bf16, False)] * 2,
        place, rows_t, teacher_scale, proto_scale, teacher_exp, student_proto, name="proto_grads_send",
    )
    from_far, from_near = flip(send_far, "c"), flip(send_near, "c")
    keep_near, keep_far = call(
        lambda *refs: proto_kernel(0, *refs),
        [((1024, D), f32, False)] * 2,
        place, rows_t, teacher_scale, proto_scale, teacher_exp, student_proto, name="proto_grads_keep",
    )
    far = flip((keep_far + from_far.astype(f32)).astype(bf16), "zl")
    losses = over_token_groups(loss)
    loss = ((losses[0] + losses[1]) + (losses[2] + losses[3]))[0, 0]
    own, one, two, three = call(
        fold_x_kernel, [((128, D), f32, False)] + [((128, D), bf16, False)] * 3,
        place, own, one, two, three, name="fold_x",
    )
    one, two, three = shift(one, "y", 1), shift(two, "y", 2), shift(three, "y", 3)
    own, send = call(
        fold_y_kernel, [((64, D), f32, False), ((64, D), bf16, False)],
        place, own, one, two, three, name="fold_y",
    )
    (feature_grads,) = call(
        feature_grads_kernel, [((64, D), f32, False)], student_rows, own, flip(send, "zh"), name="feature_grads"
    )
    chunk = lax.dynamic_slice_in_dim(student_weight, (zh * 4 + zl * 2 + c) * 1024, 1024, 0)
    (weight_grads,) = call(
        weight_grads_kernel, [((1024, D), f32, False)], place, chunk, keep_near, from_near, far,
        name="weight_grads",
    )
    return loss, feature_grads.reshape(2, 32, D), weight_grads


def solution(mesh):
    fine = Mesh(mesh.devices.reshape(2, 2, 2, 4, 4), ("zh", "zl", "c", "y", "x"))
    every = ("zh", "zl", "c", "y", "x")
    proto = ("y", "x")
    return jax.shard_map(
        local,
        mesh=fine,
        in_specs=(
            P(every, None, None),
            P(every, None, None),
            P(every, None),
            P(every, None),
            P(proto, None),
            P(proto, None),
        ),
        out_specs=(P(), P(every, None, None), P(("y", "x", "zh", "zl", "c"), None)),
        check_vma=False,
    )
```

```python
import jax
import jax.numpy as jnp
from jax import lax
from jax.experimental import pallas as pl
from jax.experimental.pallas import tpu as pltpu
from jax.sharding import Mesh, PartitionSpec as P

teacher_temp = 0.07
student_temp = 0.1
epsilon = 1e-06
LOG2E = 1.4426950408889634
SWEEPS = 3
TOKENS = 8192
T, K, D = 2048, 4096, 256
BLOCK = 512
LANES = 128
f32, bf16 = jnp.float32, jnp.bfloat16
SAME_TOKENS = ("x", "y", "zh")
VMEM = pl.BlockSpec(memory_space=pltpu.VMEM)
SMEM = pl.BlockSpec(memory_space=pltpu.SMEM)
DMA = pltpu.SemaphoreType.DMA


def nt(left, right):
    return lax.dot_general(left, right, (((1,), (1,)), ((), ())), preferred_element_type=f32)


def nn(left, right):
    return lax.dot_general(left, right, (((1,), (0,)), ((), ())), preferred_element_type=f32)


def normalize_rows(values):
    scale = lax.rsqrt(jnp.sum(values * values, axis=-1, keepdims=True) + epsilon)
    return values * scale, scale


def three_rows(row):
    high = row.astype(bf16).astype(f32)
    rest = row - high
    middle = rest.astype(bf16).astype(f32)
    low = rest - middle
    index = lax.broadcasted_iota(jnp.int32, (16, row.shape[1]), 0)
    picked = jnp.where(index == 0, high, jnp.where(index == 1, middle, jnp.where(index == 2, low, 0.0)))
    return picked.astype(bf16)


def as_row(packed):
    return jnp.concatenate([packed[j : j + 1, :] for j in range(packed.shape[0])], axis=1)


def store_packed(ref, start, row):
    for j in range(row.shape[1] // LANES):
        ref[start + j : start + j + 1, :] = row[:, j * LANES : (j + 1) * LANES]


class Far:
    def __init__(self, value):
        self.value = value


def call(kernel, outs, *args, scratch=(), limit=16, name=None, flops=0, moved=0, exps=0):
    operands, in_specs = [], []
    for arg in args:
        if isinstance(arg, Far):
            operands.append(pltpu.with_memory_space_constraint(arg.value, pltpu.HBM))
            in_specs.append(pl.BlockSpec(memory_space=pl.ANY))
        else:
            operands.append(arg)
            in_specs.append(SMEM if arg.dtype == jnp.int32 and arg.ndim == 1 else VMEM)
    shapes, out_specs = [], []
    for out in outs:
        if isinstance(out, Far):
            shapes.append(pltpu.HBM(out.value.shape, out.value.dtype))
            out_specs.append(pl.BlockSpec(memory_space=pl.ANY))
        else:
            shapes.append(out)
            out_specs.append(VMEM)
    return pl.pallas_call(
        kernel,
        out_shape=shapes,
        in_specs=in_specs,
        out_specs=out_specs,
        scratch_shapes=list(scratch),
        compiler_params=pltpu.CompilerParams(vmem_limit_bytes=limit << 20),
        cost_estimate=pl.CostEstimate(flops=flops, bytes_accessed=moved, transcendentals=exps),
        name=name,
    )(*operands)


def row_block(ref, start, size=512):
    return ref.at[pl.ds(start, size), :]


def call_blocks(
    kernel, steps, outs, in_specs, out_specs, *args, scratch=(), limit=20, name=None, flops=0, moved=0, exps=0
):
    pinned = [
        pltpu.with_memory_space_constraint(arg, pltpu.HBM) if arg.size * arg.dtype.itemsize >= 1 << 20 else arg
        for arg in args
    ]
    return pl.pallas_call(
        kernel,
        out_shape=outs,
        grid_spec=pltpu.PrefetchScalarGridSpec(
            num_scalar_prefetch=1,
            grid=(steps,),
            in_specs=in_specs,
            out_specs=out_specs,
            scratch_shapes=list(scratch),
        ),
        compiler_params=pltpu.CompilerParams(vmem_limit_bytes=limit << 20),
        cost_estimate=pl.CostEstimate(flops=flops, bytes_accessed=moved, transcendentals=exps),
        name=name,
    )(*pinned)


def lane_sums(values):
    part = values[:, 0:LANES]
    for j in range(1, values.shape[1] // LANES):
        part = part + values[:, j * LANES : (j + 1) * LANES]
    return jnp.sum(jnp.transpose(part), axis=0, keepdims=True)


def pick_rows(patches_ref, positions_ref, image):
    patch = lax.broadcasted_iota(jnp.int32, (256, 32), 0)
    chosen = (patch == positions_ref[image : image + 1, :]).astype(f32).astype(bf16)
    return lax.dot_general(chosen, patches_ref[image], (((0,), (0,)), ((), ())), preferred_element_type=f32)


def teacher_rows_kernel(patches_ref, positions_ref, copies_ref):
    for image in range(2):
        unit = normalize_rows(pick_rows(patches_ref, positions_ref, image))[0].astype(bf16)
        for copy in range(32):
            copies_ref[copy, image * 32 : (image + 1) * 32, :] = unit


def student_rows_kernel(patches_ref, positions_ref, weight_ref, copies_ref, rows_ref):
    for image in range(2):
        here = slice(image * 32, (image + 1) * 32)
        rows = pick_rows(patches_ref, positions_ref, image)
        rows_ref[here, :] = rows
        unit = normalize_rows(rows)[0].astype(bf16)
        for copy in range(32):
            copies_ref[copy, here, :] = unit
    for copy in range(32):
        copies_ref[copy, 64:80, :] = weight_ref[...]


def protos_kernel(place_ref, teacher_ref, student_ref, teacher_out_ref, student_out_ref, student_t_ref):
    teacher_out_ref[...] = normalize_rows(teacher_ref[...].astype(f32))[0].astype(bf16)
    student = normalize_rows(student_ref[...].astype(f32))[0].astype(bf16)
    student_out_ref[...] = student
    student_t_ref[...] = jnp.transpose(student.astype(f32)).astype(bf16)


def teacher_kernel(rows_ref, protos_ref, exp_ref, mass_ref, near_ref, arrived):
    steps = range(K // BLOCK)
    reads = [
        pltpu.make_async_copy(row_block(protos_ref, b * BLOCK), row_block(near_ref, b * BLOCK), arrived.at[b])
        for b in steps
    ]
    for read in reads:
        read.start()
    rows = rows_ref[...].reshape(T, D)
    for b in steps:
        here = slice(b * BLOCK, (b + 1) * BLOCK)
        reads[b].wait()
        values = jnp.exp2(nt(near_ref[here, :], rows) * (LOG2E / teacher_temp))
        exp_ref[here, :] = values.astype(bf16)
        store_packed(mass_ref, b * BLOCK // LANES, lane_sums(values))


def student_kernel(
    gathered_ref, protos_ref, far_ref, total_ref, far_rows_t_ref, weight_ref,
    rows_ref, extra_ref, near_ref, exp_ref, rows_t_ref, arrived, sent
):
    steps = range(K // BLOCK)
    get_rows = pltpu.make_async_copy(gathered_ref.at[:, pl.ds(0, 64), :], rows_ref, arrived.at[8])
    get_extra = pltpu.make_async_copy(gathered_ref.at[:, pl.ds(64, 16), :], extra_ref, arrived.at[9])
    reads = [
        pltpu.make_async_copy(row_block(protos_ref, b * BLOCK), row_block(near_ref, b * BLOCK), arrived.at[b])
        for b in steps
    ]
    writes = [
        pltpu.make_async_copy(exp_ref.at[b % 3], row_block(far_ref, b * BLOCK), sent.at[b]) for b in steps
    ]
    write_t = pltpu.make_async_copy(rows_t_ref, far_rows_t_ref, sent.at[8])
    get_rows.start()
    for read in reads:
        read.start()
    get_extra.start()
    get_rows.wait()
    rows = rows_ref[...].reshape(T, D)
    total = jnp.zeros((8, T), f32)
    for b in steps:
        reads[b].wait()
        values = jnp.exp2(nt(near_ref[b * BLOCK : (b + 1) * BLOCK, :], rows) * (LOG2E / student_temp))
        if b >= 3:
            writes[b - 3].wait()
        exp_ref[b % 3] = values.astype(bf16)
        writes[b].start()
        total = total + jnp.sum(values.reshape(BLOCK // 8, 8, T), axis=0)
    store_packed(total_ref, 0, jnp.sum(total, axis=0, keepdims=True))
    rows_t_ref[...] = jnp.transpose(rows.astype(f32)).astype(bf16)
    write_t.start()
    get_extra.wait()
    for j in range(16):
        row = jnp.zeros((1, LANES), f32)
        for piece in range(4):
            block = extra_ref[2 * j + piece // 2, :, 0:LANES].astype(f32)
            row = row + pltpu.roll(block, piece * 32, 1)[piece % 2 : piece % 2 + 1]
        weight_ref[j : j + 1, :] = row
    for b in steps[-3:]:
        writes[b].wait()
    write_t.wait()


def student_grads_kernel(
    total_ref, weight_ref, far_rows_t_ref, far_protos_t_ref, far_ref, far_unit_ref, far_proto_ref,
    rows_t_ref, protos_t_ref, exp_ref, unit_ref, proto_ref, arrived, sent
):
    steps = range(K // BLOCK)
    get_rows = pltpu.make_async_copy(far_rows_t_ref, rows_t_ref, arrived.at[8])
    get_protos = pltpu.make_async_copy(far_protos_t_ref, protos_t_ref, arrived.at[9])
    reads = [
        pltpu.make_async_copy(row_block(far_ref, b * BLOCK), row_block(exp_ref, b * BLOCK), arrived.at[b])
        for b in steps
    ]
    writes = [
        pltpu.make_async_copy(row_block(proto_ref, b * BLOCK), row_block(far_proto_ref, b * BLOCK), sent.at[b])
        for b in steps
    ]
    get_rows.start()
    for read in reads[:3]:
        read.start()
    scale = as_row(weight_ref[...] / (student_temp * total_ref[...]))
    get_rows.wait()
    right = (rows_t_ref[...].astype(f32) * scale).astype(bf16)
    for b in steps:
        here = slice(b * BLOCK, (b + 1) * BLOCK)
        reads[b].wait()
        following = (reads + [get_protos])[b + 3 : b + 4]
        for read in following:
            read.start()
        proto_ref[here, :] = nt(exp_ref[here, :], right)
        writes[b].start()
    get_protos.wait()
    unit_writes = []
    for j in range(T // BLOCK):
        here = slice(j * BLOCK, (j + 1) * BLOCK)
        unit_ref[:, here] = nn(protos_t_ref[...], exp_ref[:, here])
        lanes = pl.ds(j * BLOCK, BLOCK)
        write = pltpu.make_async_copy(unit_ref.at[:, lanes], far_unit_ref.at[:, lanes], sent.at[8 + j])
        write.start()
        unit_writes.append(write)
    for write in writes + unit_writes:
        write.wait()


def proto_scale_of(own_ref, core_ref, z_ref, both_ref):
    return 1.0 / ((own_ref[...] + core_ref[...]) + (z_ref[...] + both_ref[...]))


def store_copies(ref, start, row):
    for j in range(row.shape[1] // LANES):
        piece = row[:, j * LANES : (j + 1) * LANES]
        for copy in range(32):
            ref[copy, start + j : start + j + 1, :] = piece


def first_token_mass_kernel(own_ref, core_ref, z_ref, both_ref, exp_ref, mass_ref):
    scale = three_rows(as_row(proto_scale_of(own_ref, core_ref, z_ref, both_ref)))
    total = jnp.zeros((16, T), f32)
    for b in range(K // BLOCK):
        here = slice(b * BLOCK, (b + 1) * BLOCK)
        total = total + nn(scale[:, here], exp_ref[here, :])
    store_copies(mass_ref, 0, jnp.sum(total, axis=0, keepdims=True))


def token_mass_kernel(own_ref, core_ref, z_ref, both_ref, exp_ref, student_ref, mass_ref):
    scale = three_rows(as_row(proto_scale_of(own_ref, core_ref, z_ref, both_ref)))
    total = jnp.zeros((16, T), f32)
    for b in range(K // BLOCK):
        here = slice(b * BLOCK, (b + 1) * BLOCK)
        total = total + nn(scale[:, here], exp_ref[here, :])
    store_copies(mass_ref, 0, jnp.sum(total, axis=0, keepdims=True))
    student = student_ref[...]
    for copy in range(32):
        mass_ref[copy, 16:32, :] = student


def last_token_mass_kernel(
    own_ref, core_ref, z_ref, both_ref, exp_ref, protos_t_ref, rows_t_ref,
    mass_ref, scale_ref, far_grads_ref, left_ref, grads_ref, sent
):
    packed = proto_scale_of(own_ref, core_ref, z_ref, both_ref)
    scale_ref[...] = packed
    scale = as_row(packed)
    left_ref[D : D + 16, :] = three_rows(scale)
    left_ref[0:D, :] = (protos_t_ref[...].astype(f32) * scale).astype(bf16)
    writes = []
    for j in range(T // BLOCK):
        here = slice(j * BLOCK, (j + 1) * BLOCK)
        both = nn(left_ref[...], exp_ref[:, here])
        grads = both[0:D]
        grads_ref[:, here] = grads
        lanes = pl.ds(j * BLOCK, BLOCK)
        write = pltpu.make_async_copy(grads_ref.at[:, lanes], far_grads_ref.at[:, lanes], sent.at[j])
        write.start()
        writes.append(write)
        store_copies(mass_ref, j * BLOCK // LANES, jnp.sum(both[D:], axis=0, keepdims=True))
        cross = jnp.sum(grads * rows_t_ref[:, here].astype(f32), axis=0, keepdims=True)
        store_copies(mass_ref, (T + j * BLOCK) // LANES, cross)
    for write in writes:
        write.wait()


def column_mass(scale, exp_ref, mass_ref, arrive=None):
    for b in range(K // BLOCK):
        if arrive is not None:
            arrive(b)
        part = jnp.zeros((BLOCK, LANES), f32)
        for j in range(T // LANES):
            lanes = slice(j * LANES, (j + 1) * LANES)
            part = part + exp_ref[b * BLOCK : (b + 1) * BLOCK, lanes].astype(f32) * scale[:, lanes]
        row = jnp.sum(jnp.transpose(part), axis=0, keepdims=True)
        store_packed(mass_ref, b * BLOCK // LANES, row)


def first_proto_mass_kernel(parts_ref, far_ref, exp_ref, mass_ref, arrived):
    def block_copy(b):
        here = pl.ds(b * BLOCK, BLOCK)
        return pltpu.make_async_copy(far_ref.at[here, :], exp_ref.at[here, :], arrived.at[b])

    for b in range(K // BLOCK):
        block_copy(b).start()
    scale = 1.0 / as_row(jnp.sum(parts_ref[...], axis=0))
    column_mass(scale, exp_ref, mass_ref, lambda b: block_copy(b).wait())


def proto_mass_kernel(parts_ref, exp_ref, mass_ref, total_ref):
    parts = jnp.sum(parts_ref[...], axis=0)
    total_ref[...] = parts[16:32]
    column_mass(1.0 / as_row(parts[0:16]), exp_ref, mass_ref)


def combine_kernel(
    parts_ref, total_ref, weight_ref, far_student_ref, far_teacher_ref,
    loss_ref, scale_ref, grads_ref, student_ref, teacher_ref, arrived
):
    reads = []
    for j in range(T // BLOCK):
        lanes = pl.ds(j * BLOCK, BLOCK)
        for k, (far, near) in enumerate(((far_student_ref, student_ref), (far_teacher_ref, teacher_ref))):
            reads.append(pltpu.make_async_copy(far.at[:, lanes], near.at[:, lanes], arrived.at[2 * j + k]))
    for read in reads:
        read.start()
    parts = jnp.sum(parts_ref[...], axis=0)
    token_scale = 1.0 / parts[0:16]
    total, weight = total_ref[...], weight_ref[...]
    cross = jnp.log(total) - token_scale * parts[16:32] / student_temp
    loss_ref[...] = jnp.full((8, LANES), jnp.sum(weight * cross) / TOKENS, f32)
    teacher_scale = weight * token_scale / student_temp
    scale_ref[...] = teacher_scale
    student_row = as_row(weight / (student_temp * total))
    teacher_row = as_row(teacher_scale)
    for j in range(T // BLOCK):
        here = slice(j * BLOCK, (j + 1) * BLOCK)
        reads[2 * j].wait()
        reads[2 * j + 1].wait()
        grads = student_ref[:, here] * student_row[:, here] - teacher_ref[:, here] * teacher_row[:, here]
        grads = jnp.transpose(grads).astype(bf16)
        for k in range(BLOCK // 64):
            grads_ref[j * (BLOCK // 64) + k] = grads[k * 64 : (k + 1) * 64]


def proto_kernel(
    chunks, place_ref, loss_ref, teacher_scale_ref, scale_ref, far_rows_t_ref, far_exp_ref, far_student_ref, *refs
):
    outs, (rows_t_ref, exp_ref, student_ref, arrived) = refs[: len(chunks)], refs[len(chunks) :]
    get_rows = pltpu.make_async_copy(far_rows_t_ref, rows_t_ref, arrived.at[0])
    get_rows.start()
    reads, rows = [], []
    for i, (z_flip, core_flip) in enumerate(chunks):
        z = 1 - place_ref[1] if z_flip else place_ref[1]
        core = 1 - place_ref[2] if core_flip else place_ref[2]
        for b in range(2):
            start = pl.multiple_of((z * 2 + core) * 1024 + b * 512, 512)
            slot = 2 * i + b
            rows.append((z * 2 + core) * 8 + b * 4)
            reads.append((
                pltpu.make_async_copy(
                    row_block(far_exp_ref, start), row_block(exp_ref, slot * 512), arrived.at[1 + 2 * slot]
                ),
                pltpu.make_async_copy(
                    row_block(far_student_ref, start), row_block(student_ref, slot * 512), arrived.at[2 + 2 * slot]
                ),
            ))
    for pair in reads:
        for read in pair:
            read.start()
    if outs[0].shape[0] > 1024:
        outs[0][1024:1040, :] = loss_rows(loss_ref[0:1, :])
    get_rows.wait()
    right = (rows_t_ref[...].astype(f32) * as_row(teacher_scale_ref[...])).astype(bf16)
    for slot, pair in enumerate(reads):
        for read in pair:
            read.wait()
        product = nt(exp_ref[slot * 512 : (slot + 1) * 512, :], right)
        ref = outs[slot // 2]
        for j in range(4):
            row = scale_ref[pl.ds(rows[slot] + j, 1), :]
            column = jnp.transpose(jnp.broadcast_to(row, (LANES, LANES)))
            column = jnp.concatenate([column, column], axis=1)
            start = slot * 512 + j * LANES
            value = student_ref[start : start + LANES, :] - product[j * LANES : (j + 1) * LANES] * column
            start -= slot // 2 * 1024
            ref[start : start + LANES, :] = value.astype(ref.dtype)


def loss_rows(row):
    return three_rows(jnp.concatenate([row, row], axis=1))


def loss_of(rows):
    return jnp.sum(rows.astype(f32), axis=0, keepdims=True)[:, 0:LANES]


def fold_kernel(own_ref, core_ref, loss_ref, first_ref, second_ref, loss_out_ref):
    loss = loss_ref[0:1, :] + loss_of(core_ref[1024:1040, :])
    loss_out_ref[...] = jnp.broadcast_to(loss, (8, LANES))
    first_ref[512:528, :] = loss_rows(loss)
    first_ref[0:512, :] = (own_ref[0:512, :] + core_ref[0:512, :].astype(f32)).astype(bf16)
    second_ref[...] = (own_ref[512:1024, :] + core_ref[512:1024, :].astype(f32)).astype(bf16)


def normalize_back(unit, scale, grad):
    return scale * (grad - unit * jnp.sum(unit * grad, axis=-1, keepdims=True))


def weight_grads_kernel(
    place_ref, loss_ref, far_weight_ref, far_own_ref, core_ref, first_ref, second_ref,
    out_ref, loss_out_ref, weight_ref, own_ref, arrived
):
    chunk = place_ref[0] * 4 + place_ref[1] * 2 + place_ref[2]
    start = pl.multiple_of(chunk * 1024, 1024)
    get_weight = pltpu.make_async_copy(row_block(far_weight_ref, start, 1024), weight_ref, arrived.at[0])
    get_own = pltpu.make_async_copy(far_own_ref, own_ref, arrived.at[1])
    get_weight.start()
    get_own.start()
    loss_out_ref[...] = (loss_ref[0:1, :] + loss_of(first_ref[512:528, :]))[:, 0:1]
    get_weight.wait()
    get_own.wait()
    for half, far_ref in enumerate((first_ref, second_ref)):
        here = slice(half * 512, (half + 1) * 512)
        grads = own_ref[here, :] + core_ref[here, :].astype(f32) + far_ref[0:512, :].astype(f32)
        unit, scale = normalize_rows(weight_ref[here, :].astype(f32))
        out_ref[here, :] = normalize_back(unit, scale, grads)


def feature_grads_kernel(rows_ref, parts_ref, out_ref):
    grads = parts_ref[0].astype(f32)
    for j in range(1, 32):
        grads = grads + parts_ref[j].astype(f32)
    unit, scale = normalize_rows(rows_ref[...])
    out_ref[...] = normalize_back(unit, scale, grads)


def flip(values, axis):
    return lax.ppermute(values, axis, [(0, 1), (1, 0)])


def flip_both(values):
    return lax.ppermute(values, ("zl", "c"), [(i, 3 - i) for i in range(4)])


def over_token_groups(values):
    return values, flip(values, "c"), flip(values, "zl"), flip_both(values)


def exchange(blocks):
    return lax.all_to_all(blocks, SAME_TOKENS, 0, 0, tiled=True)


def local(student_patches, teacher_patches, mask_positions, token_weight, student_weight, teacher_weight):
    zh, zl, c, y, x = (lax.axis_index(name) for name in ("zh", "zl", "c", "y", "x"))
    place = jnp.stack([zh, zl, c, y, x]).astype(jnp.int32)
    matrix = K * T * 2
    product = 2 * K * T * D
    blocks = K // BLOCK
    shape = jax.ShapeDtypeStruct
    row, rows = shape((16, LANES), f32), shape((32, LANES), f32)
    half = pl.BlockSpec((BLOCK, D), lambda i, place: (place[0] * blocks + i, 0))
    block = pl.BlockSpec((BLOCK, D), lambda i, place: (i, 0))
    column = pl.BlockSpec((D, BLOCK), lambda i, place: (0, i))

    (copies,) = call(
        teacher_rows_kernel, [shape((32, 64, D), bf16)], teacher_patches, mask_positions,
        name="teacher_rows", moved=1 << 20,
    )
    teacher_all = exchange(copies)
    copies, student_rows = call(
        student_rows_kernel, [shape((32, 80, D), bf16), shape((64, D), f32)],
        student_patches, mask_positions, jnp.pad(token_weight, ((0, 14), (0, 224))),
        name="student_rows", moved=1 << 20,
    )
    teacher_protos, student_protos, protos_t = call_blocks(
        protos_kernel, blocks,
        [pltpu.HBM((K, D), bf16), pltpu.HBM((K, D), bf16), pltpu.HBM((D, K), bf16)],
        [half, half], [block, block, column],
        place, teacher_weight, student_weight, name="protos", moved=5 * K * D * 2,
    )
    copies, teacher_all, teacher_protos, student_protos = lax.optimization_barrier(
        (copies, teacher_all, teacher_protos, student_protos)
    )
    student_all = exchange(copies)
    teacher_near, mass = call(
        teacher_kernel, [pltpu.VMEM((K, T), bf16), rows], teacher_all, Far(teacher_protos),
        scratch=[pltpu.VMEM((K, D), bf16), DMA((blocks,))],
        name="teacher_exp", flops=product, moved=matrix, exps=K * T,
    )
    masses = over_token_groups(mass)
    (copies,) = call(
        first_token_mass_kernel, [shape((32, 16, LANES), f32)], *masses, teacher_near,
        name="token_mass", moved=matrix // 2,
    )
    copies, student_all = lax.optimization_barrier((copies, student_all))
    parts = exchange(copies)
    student_exp, total, rows_t, weight = call(
        student_kernel, [Far(shape((K, T), bf16)), row, Far(shape((D, T), bf16)), row],
        Far(student_all), Far(student_protos),
        scratch=[
            pltpu.VMEM((32, 64, D), bf16), pltpu.VMEM((32, 16, D), bf16), pltpu.VMEM((K, D), bf16),
            pltpu.VMEM((3, BLOCK, T), bf16), pltpu.VMEM((D, T), bf16), DMA((10,)), DMA((9,)),
        ],
        limit=32, name="student_exp", flops=product, moved=matrix, exps=K * T,
    )
    parts, total = lax.optimization_barrier((parts, total))
    resident, mass = call(
        first_proto_mass_kernel, [pltpu.VMEM((K, T), bf16), rows], parts, Far(teacher_near),
        scratch=[DMA((blocks,))], name="proto_mass", moved=matrix,
    )
    masses = over_token_groups(mass)
    (copies,) = call(
        token_mass_kernel, [shape((32, 32, LANES), f32)], *masses, resident, total,
        name="token_mass", moved=matrix // 2,
    )
    parts = exchange(copies)
    mass, total = call(
        proto_mass_kernel, [rows, row], parts, resident, name="proto_mass", moved=matrix // 2
    )
    masses = over_token_groups(mass)
    copies, proto_scale, teacher_part = call(
        last_token_mass_kernel,
        [shape((32, 32, LANES), f32), rows, Far(shape((D, T), f32))],
        *masses, resident, protos_t, rows_t,
        scratch=[pltpu.VMEM((D + 16, K), bf16), pltpu.VMEM((D, T), f32), DMA((4,))],
        limit=20, name="last_token_mass", flops=product, moved=matrix,
    )
    parts = exchange(copies)
    student_part, student_proto = call(
        student_grads_kernel, [Far(shape((D, T), f32)), Far(shape((K, D), f32))],
        total, weight, Far(rows_t), Far(protos_t), Far(student_exp),
        scratch=[
            pltpu.VMEM((D, T), bf16), pltpu.VMEM((D, K), bf16), pltpu.VMEM((K, T), bf16),
            pltpu.VMEM((D, T), f32), pltpu.VMEM((K, D), f32), DMA((10,)), DMA((12,)),
        ],
        limit=40, name="student_grads", flops=2 * product, moved=matrix,
    )
    loss, teacher_scale, copies = call(
        combine_kernel, [shape((8, LANES), f32), row, shape((32, 64, D), bf16)],
        parts, total, weight, Far(student_part), Far(teacher_part),
        scratch=[pltpu.VMEM((D, T), f32), pltpu.VMEM((D, T), f32), DMA((8,))],
        name="combine", moved=6 << 20,
    )
    unit_parts = exchange(copies)

    def proto_grads(name, chunks, outs):
        count = len(chunks)
        return call(
            lambda *refs: proto_kernel(chunks, *refs), outs,
            place, loss, teacher_scale, proto_scale, Far(rows_t), Far(teacher_near), Far(student_proto),
            scratch=[
                pltpu.VMEM((D, T), bf16), pltpu.VMEM((count * 1024, T), bf16),
                pltpu.VMEM((count * 1024, D), f32), DMA((1 + 4 * count,)),
            ],
            limit=24, name=name, flops=product * count // 4, moved=matrix * count // 4,
        )

    keep = shape((1024, D), f32)
    (send_far,) = proto_grads("proto_grads_send_far", [(True, True)], [shape((1040, D), bf16)])
    from_far = flip(send_far, "c")
    (keep_far,) = proto_grads("proto_grads_keep_far", [(True, False)], [keep])
    first, second, loss_here = call(
        fold_kernel, [shape((528, D), bf16), shape((512, D), bf16), shape((8, LANES), f32)],
        keep_far, from_far, loss, name="fold", moved=1 << 20,
    )
    first_there, second_there = flip(first, "zl"), flip(second, "zl")
    send_near, keep_near = proto_grads(
        "proto_grads_near", [(False, True), (False, False)], [shape((1024, D), bf16), keep]
    )
    from_near = flip(send_near, "c")
    (feature_grads,) = call(
        feature_grads_kernel, [shape((64, D), f32)], student_rows, unit_parts, name="feature_grads", moved=1 << 20,
    )
    weight_grads, loss = call(
        weight_grads_kernel, [keep, shape((1, 1), f32)],
        place, loss_here, Far(student_weight), Far(keep_near), from_near, first_there, second_there,
        scratch=[pltpu.VMEM((1024, D), bf16), pltpu.VMEM((1024, D), f32), DMA((2,))],
        name="weight_grads", moved=3 << 20,
    )
    return loss.reshape(()), feature_grads.reshape(2, 32, D), weight_grads


def solution(mesh):
    fine = Mesh(mesh.devices.reshape(2, 2, 2, 4, 4), ("zh", "zl", "c", "y", "x"))
    every = ("zh", "zl", "c", "y", "x")
    proto = ("y", "x")
    return jax.shard_map(
        local,
        mesh=fine,
        in_specs=(
            P(every, None, None),
            P(every, None, None),
            P(every, None),
            P(every, None),
            P(proto, None),
            P(proto, None),
        ),
        out_specs=(P(), P(every, None, None), P(("y", "x", "zh", "zl", "c"), None)),
        check_vma=False,
    )
```

```python
import jax
import jax.numpy as jnp
from jax import lax
from jax.experimental import pallas as pl
from jax.experimental.pallas import tpu as pltpu
from jax.sharding import Mesh, PartitionSpec as P

teacher_temp = 0.07
student_temp = 0.1
epsilon = 1e-06
LOG2E = 1.4426950408889634
SWEEPS = 3
TOKENS = 8192
T, K, D = 1024, 8192, 256
BLOCK = 512
LANES = 128
f32, bf16 = jnp.float32, jnp.bfloat16
GROUPS = 16
PACKED = T // LANES
SAME_TOKENS = ("y", "x")
VMEM = pl.BlockSpec(memory_space=pltpu.VMEM)
SMEM = pl.BlockSpec(memory_space=pltpu.SMEM)


def nt(left, right):
    return lax.dot_general(left, right, (((1,), (1,)), ((), ())), preferred_element_type=f32)


def nn(left, right):
    return lax.dot_general(left, right, (((1,), (0,)), ((), ())), preferred_element_type=f32)


def normalize_rows(values):
    scale = lax.rsqrt(jnp.sum(values * values, axis=-1, keepdims=True) + epsilon)
    return values * scale, scale


def three_rows(row):
    high = row.astype(bf16).astype(f32)
    rest = row - high
    middle = rest.astype(bf16).astype(f32)
    low = rest - middle
    index = lax.broadcasted_iota(jnp.int32, (16, row.shape[1]), 0)
    picked = jnp.where(index == 0, high, jnp.where(index == 1, middle, jnp.where(index == 2, low, 0.0)))
    return picked.astype(bf16)


def as_row(packed):
    return jnp.concatenate([packed[j : j + 1, :] for j in range(packed.shape[0])], axis=1)


def store_packed(ref, start, row):
    for j in range(row.shape[1] // LANES):
        ref[start + j : start + j + 1, :] = row[:, j * LANES : (j + 1) * LANES]


def call(kernel, outs, *args, far=(), scratch=(), limit=11, name=None, flops=0, moved=0, exps=0):
    specs = [SMEM if arg.dtype == jnp.int32 and arg.ndim == 1 else VMEM for arg in args]
    args = list(args)
    for i in far:
        specs[i] = pl.BlockSpec(memory_space=pl.ANY)
        args[i] = pltpu.with_memory_space_constraint(args[i], pltpu.HBM)
    return pl.pallas_call(
        kernel,
        out_shape=outs,
        in_specs=specs,
        out_specs=[VMEM] * len(outs),
        scratch_shapes=list(scratch),
        compiler_params=pltpu.CompilerParams(vmem_limit_bytes=limit << 20),
        cost_estimate=pl.CostEstimate(flops=flops, bytes_accessed=moved, transcendentals=exps),
        name=name,
    )(*args)


def lane_sums(values):
    part = values[:, 0:LANES]
    for j in range(1, values.shape[1] // LANES):
        part = part + values[:, j * LANES : (j + 1) * LANES]
    return jnp.sum(jnp.transpose(part), axis=0, keepdims=True)


def pick_rows(patches_ref, positions_ref, image):
    patch = lax.broadcasted_iota(jnp.int32, (256, 32), 0)
    chosen = (patch == positions_ref[image : image + 1, :]).astype(f32).astype(bf16)
    return lax.dot_general(chosen, patches_ref[image], (((0,), (0,)), ((), ())), preferred_element_type=f32)


def rows_kernel(
    far_teacher_ref, far_student_ref, positions_ref, weight_ref, copies_ref, rows_ref, teacher_ref, student_ref, arrived
):
    reads = []
    for i, (far, near) in enumerate(((far_teacher_ref, teacher_ref), (far_student_ref, student_ref))):
        reads.append(pltpu.make_async_copy(far, near, arrived.at[i]))
        reads[i].start()
    row = lax.broadcasted_iota(jnp.int32, (16, 32), 0)
    weight = weight_ref[...].astype(f32)
    weight = jnp.where(row == 0, weight[0:1], jnp.where(row == 1, weight[1:2], 0.0)).astype(bf16)
    same = lax.broadcasted_iota(jnp.int32, (32, D), 0) == lax.broadcasted_iota(jnp.int32, (32, D), 1)
    weight = nn(weight, same.astype(f32).astype(bf16)).astype(bf16)
    for copy in range(GROUPS):
        copies_ref[copy, 128:144, :] = weight
    for read in reads:
        read.wait()
    for image in range(2):
        teacher = normalize_rows(pick_rows(teacher_ref, positions_ref, image))[0].astype(bf16)
        rows = pick_rows(student_ref, positions_ref, image)
        rows_ref[image * 32 : (image + 1) * 32, :] = rows
        student = normalize_rows(rows)[0].astype(bf16)
        for copy in range(GROUPS):
            copies_ref[copy, image * 32 : (image + 1) * 32, :] = teacher
            copies_ref[copy, 64 + image * 32 : 64 + (image + 1) * 32, :] = student


def teacher_kernel(gathered_ref, weight_ref, exp_ref, mass_ref):
    rows = gathered_ref[:, 0:64, :].reshape(T, D)
    for b in range(K // BLOCK):
        here = slice(b * BLOCK, (b + 1) * BLOCK)
        protos = normalize_rows(weight_ref[here, :].astype(f32))[0].astype(bf16)
        values = jnp.exp2(nt(protos, rows) * (LOG2E / teacher_temp))
        exp_ref[here, :] = values.astype(bf16)
        store_packed(mass_ref, b * BLOCK // LANES, lane_sums(values))


def student_kernel(gathered_ref, weight_ref, exp_ref, total_ref, protos_t_ref, rows_t_ref, token_weight_ref):
    rows = gathered_ref[:, 64:128, :].reshape(T, D)
    rows_t_ref[...] = jnp.transpose(rows.astype(f32)).astype(bf16)
    for j in range(PACKED):
        row = jnp.zeros((1, LANES), f32)
        for piece in range(4):
            block = gathered_ref[2 * j + piece // 2, 128:144, 0:LANES].astype(f32)
            row = row + pltpu.roll(block, piece * 32, 1)[piece % 2 : piece % 2 + 1]
        token_weight_ref[j : j + 1, :] = row
    total = jnp.zeros((8, T), f32)
    for b in range(K // BLOCK):
        here = slice(b * BLOCK, (b + 1) * BLOCK)
        protos = normalize_rows(weight_ref[here, :].astype(f32))[0].astype(bf16)
        protos_t_ref[:, here] = jnp.transpose(protos.astype(f32)).astype(bf16)
        values = jnp.exp2(nt(protos, rows) * (LOG2E / student_temp))
        exp_ref[here, :] = values.astype(bf16)
        total = total + jnp.sum(values.reshape(BLOCK // 8, 8, T), axis=0)
    store_packed(total_ref, 0, jnp.sum(total, axis=0, keepdims=True))


def student_unit_kernel(protos_t_ref, exp_ref, out_ref):
    for j in range(T // BLOCK):
        here = slice(j * BLOCK, (j + 1) * BLOCK)
        out_ref[:, here] = nn(protos_t_ref[...], exp_ref[:, here])


def student_proto_kernel(rows_t_ref, total_ref, weight_ref, exp_ref, out_ref):
    scale = as_row(weight_ref[...] / (student_temp * total_ref[...]))
    right = (rows_t_ref[...].astype(f32) * scale).astype(bf16)
    for b in range(K // BLOCK):
        here = slice(b * BLOCK, (b + 1) * BLOCK)
        out_ref[here, :] = nt(exp_ref[here, :], right).astype(bf16)


def store_copies(ref, start, row):
    for j in range(row.shape[1] // LANES):
        piece = row[:, j * LANES : (j + 1) * LANES]
        for copy in range(GROUPS):
            ref[copy, start + j : start + j + 1, :] = piece


def token_mass(packed, exp_ref, mass_ref):
    scale = three_rows(as_row(packed))
    total = jnp.zeros((16, T), f32)
    for b in range(K // BLOCK):
        here = slice(b * BLOCK, (b + 1) * BLOCK)
        total = total + nn(scale[:, here], exp_ref[here, :])
    store_copies(mass_ref, 0, jnp.sum(total, axis=0, keepdims=True))


def first_token_mass_kernel(near_ref, far_ref, exp_ref, student_exp_ref, mass_ref):
    token_mass(1.0 / (near_ref[...] + far_ref[...]), exp_ref, mass_ref)


def token_mass_kernel(near_ref, far_ref, exp_ref, student_ref, mass_ref):
    token_mass(1.0 / (near_ref[...] + far_ref[...]), exp_ref, mass_ref)
    student = student_ref[...]
    for copy in range(GROUPS):
        mass_ref[copy, PACKED : 2 * PACKED, :] = student


def last_token_mass_kernel(
    near_ref, far_ref, exp_ref, protos_t_ref, rows_t_ref, mass_ref, scale_ref, grads_ref, left_ref
):
    packed = 1.0 / (near_ref[...] + far_ref[...])
    scale_ref[...] = packed
    scale = as_row(packed)
    left_ref[D : D + 16, :] = three_rows(scale)
    left_ref[0:D, :] = (protos_t_ref[...].astype(f32) * scale).astype(bf16)
    for j in range(T // BLOCK):
        here = slice(j * BLOCK, (j + 1) * BLOCK)
        both = nn(left_ref[...], exp_ref[:, here])
        grads = both[0:D]
        grads_ref[:, here] = grads
        store_copies(mass_ref, j * BLOCK // LANES, jnp.sum(both[D:], axis=0, keepdims=True))
        cross = jnp.sum(grads * rows_t_ref[:, here].astype(f32), axis=0, keepdims=True)
        store_copies(mass_ref, (T + j * BLOCK) // LANES, cross)


def column_mass(scale, exp_ref, mass_ref):
    for b in range(K // BLOCK):
        part = jnp.zeros((BLOCK, LANES), f32)
        for j in range(T // LANES):
            lanes = slice(j * LANES, (j + 1) * LANES)
            part = part + exp_ref[b * BLOCK : (b + 1) * BLOCK, lanes].astype(f32) * scale[:, lanes]
        row = jnp.sum(jnp.transpose(part), axis=0, keepdims=True)
        store_packed(mass_ref, b * BLOCK // LANES, row)


def first_proto_mass_kernel(parts_ref, exp_ref, mass_ref):
    column_mass(1.0 / as_row(jnp.sum(parts_ref[...], axis=0)), exp_ref, mass_ref)


def proto_mass_kernel(parts_ref, exp_ref, mass_ref, total_ref):
    parts = jnp.sum(parts_ref[...], axis=0)
    total_ref[...] = parts[PACKED:]
    column_mass(1.0 / as_row(parts[0:PACKED]), exp_ref, mass_ref)


def combine_kernel(
    place_ref, parts_ref, total_ref, weight_ref, student_ref, teacher_ref,
    loss_ref, scale_ref, keep_ref, one_ref, two_ref, three_ref, rows_ref
):
    parts = jnp.sum(parts_ref[...], axis=0)
    token_scale = 1.0 / parts[0:PACKED]
    total, weight = total_ref[...], weight_ref[...]
    cross = jnp.log(total) - token_scale * parts[PACKED:] / student_temp
    loss_ref[...] = jnp.full((8, LANES), jnp.sum(weight * cross) / TOKENS, f32)
    teacher_scale = weight * token_scale / student_temp
    scale_ref[...] = teacher_scale
    rows_ref[0:1, :] = as_row(weight / (student_temp * total))
    rows_ref[8:9, :] = as_row(teacher_scale)
    for step, ref in enumerate((keep_ref, one_ref, two_ref, three_ref)):
        block = lax.rem(place_ref[2] + step, 4)
        here = pl.ds(pl.multiple_of(block * 256, 256), 256)
        grads = student_ref[:, here] * rows_ref[0:1, here] - teacher_ref[:, here] * rows_ref[8:9, here]
        ref[...] = jnp.transpose(grads).astype(ref.dtype)


def fold_rows_kernel(place_ref, own_ref, a_ref, b_ref, c_ref, keep_ref, one_ref, two_ref, three_ref):
    for step, ref in enumerate((keep_ref, one_ref, two_ref, three_ref)):
        block = lax.rem(place_ref[3] + step, 4)
        here = pl.ds(pl.multiple_of(block * 64, 64), 64)
        total = own_ref[here, :] + a_ref[here, :].astype(f32) + b_ref[here, :].astype(f32)
        ref[...] = (total + c_ref[here, :].astype(f32)).astype(ref.dtype)


def proto_kernel(chunks, place_ref, loss_ref, teacher_scale_ref, scale_ref, rows_t_ref, exp_ref, student_ref, *outs):
    right = (rows_t_ref[...].astype(f32) * as_row(teacher_scale_ref[...])).astype(bf16)
    for (z_step, core_flip), ref in zip(chunks, outs):
        z = lax.rem(place_ref[0] + z_step, 4)
        core = 1 - place_ref[1] if core_flip else place_ref[1]
        chunk = z * 2 + core
        if ref.shape[0] > 1024:
            ref[1024:1040, :] = loss_rows(loss_ref[0:1, :])
        for b in range(2):
            start = pl.multiple_of(chunk * 1024 + b * 512, 512)
            product = nt(exp_ref[pl.ds(start, 512), :], right)
            student = student_ref[pl.ds(start, 512), :].astype(f32)
            for j in range(4):
                row = scale_ref[pl.ds(chunk * 8 + b * 4 + j, 1), :]
                column = jnp.transpose(jnp.broadcast_to(row, (LANES, LANES)))
                column = jnp.concatenate([column, column], axis=1)
                here = slice(j * LANES, (j + 1) * LANES)
                value = student[here] - product[here] * column
                ref[b * 512 + j * LANES : b * 512 + (j + 1) * LANES, :] = value.astype(ref.dtype)


def loss_rows(row):
    return three_rows(jnp.concatenate([row, row], axis=1))


def loss_of(rows):
    return jnp.sum(rows.astype(f32), axis=0, keepdims=True)[:, 0:LANES]


def first_fold_kernel(own_ref, core_ref, loss_ref, up_ref, up2_ref, down_ref, down2_ref, loss_out_ref):
    loss = loss_ref[0:1, :] + loss_of(core_ref[1024:1040, :])
    loss_out_ref[...] = jnp.broadcast_to(loss, (8, LANES))
    for i, ref in enumerate((up_ref, up2_ref, down_ref, down2_ref)):
        here = slice(i * 256, (i + 1) * 256)
        ref[0:256, :] = (own_ref[here, :] + core_ref[here, :].astype(f32)).astype(bf16)
    up_ref[256:272, :] = loss_rows(loss)
    down_ref[256:272, :] = loss_rows(loss)


def second_fold_kernel(
    next_ref, next_core_ref, last_ref, last_core_ref, up_ref, up2_ref, down_ref, down2_ref,
    next_out_ref, next2_out_ref, last_out_ref, last2_out_ref
):
    outs = (next_out_ref, next2_out_ref, last_out_ref, last2_out_ref)
    for i, (own, core) in enumerate(((next_ref, next_core_ref), (last_ref, last_core_ref))):
        for half in range(2):
            out = outs[2 * i + half]
            for part in range(2):
                here = slice(half * 512 + part * 256, half * 512 + (part + 1) * 256)
                value = own[here, :] + core[here, :].astype(f32)
                if i == half:
                    received = ((up_ref, up2_ref), (down_ref, down2_ref))[i][part]
                    value = value + received[0:256, :].astype(f32)
                out[part * 256 : (part + 1) * 256, :] = value.astype(bf16)
    next_out_ref[512:528, :] = up_ref[256:272, :]


def normalize_back(unit, scale, grad):
    return scale * (grad - unit * jnp.sum(unit * grad, axis=-1, keepdims=True))


def weight_grads_kernel(
    place_ref, far_weight_ref, own_ref, core_ref, loss_ref, up_ref, down_ref, up_first_ref, up_second_ref,
    down_first_ref, down_second_ref, out_ref, loss_out_ref, weight_ref, arrived
):
    start = pl.multiple_of((place_ref[0] * 2 + place_ref[1]) * 1024, 1024)
    read = pltpu.make_async_copy(far_weight_ref.at[pl.ds(start, 1024), :], weight_ref, arrived)
    read.start()
    far = loss_ref[0:1, :] + loss_of(up_first_ref[512:528, :])
    loss = far + (loss_of(up_ref[256:272, :]) + loss_of(down_ref[256:272, :]))
    loss_out_ref[...] = loss[:, 0:1]
    read.wait()
    for half, (up, down) in enumerate(((up_first_ref, down_first_ref), (up_second_ref, down_second_ref))):
        here = slice(half * 512, (half + 1) * 512)
        grads = own_ref[here, :] + core_ref[here, :].astype(f32)
        grads = grads + (up[0:512, :].astype(f32) + down[0:512, :].astype(f32))
        unit, scale = normalize_rows(weight_ref[here, :].astype(f32))
        out_ref[here, :] = normalize_back(unit, scale, grads)


def feature_grads_kernel(rows_ref, own_ref, a_ref, b_ref, c_ref, out_ref):
    grads = own_ref[...] + a_ref[...].astype(f32) + b_ref[...].astype(f32) + c_ref[...].astype(f32)
    unit, scale = normalize_rows(rows_ref[...])
    out_ref[...] = normalize_back(unit, scale, grads)


def turn(values, axis, step):
    return lax.ppermute(values, axis, [(i, (i + step) % 4) for i in range(4)])


def flip(values, axis):
    return lax.ppermute(values, axis, [(0, 1), (1, 0)])


def over_token_groups(values):
    pairs = [(i, i ^ 1) for i in range(4)]
    both = [(z * 2 + c, (z ^ 1) * 2 + (1 - c)) for z in range(4) for c in range(2)]
    near = (values + flip(values, "c")) + (lax.ppermute(values, "z", pairs) + lax.ppermute(values, ("z", "c"), both))
    return near, lax.ppermute(near, "z", [(i, 3 - i) for i in range(4)])


def exchange(blocks):
    return lax.all_to_all(blocks, SAME_TOKENS, 0, 0, tiled=True)


def local(student_patches, teacher_patches, mask_positions, token_weight, student_weight, teacher_weight):
    z, c, y, x = (lax.axis_index(name) for name in ("z", "c", "y", "x"))
    place = jnp.stack([z, c, y, x]).astype(jnp.int32)
    matrix = K * T * 2
    product = 2 * K * T * D
    shape = jax.ShapeDtypeStruct
    row, rows = shape((PACKED, LANES), f32), shape((K // LANES, LANES), f32)
    resident = pltpu.VMEM((K, T), bf16)

    copies, student_rows = call(
        rows_kernel, [shape((GROUPS, 144, D), bf16), shape((64, D), f32)],
        teacher_patches, student_patches, mask_positions, token_weight, far=(0, 1),
        scratch=[pltpu.VMEM((2, 256, D), bf16), pltpu.VMEM((2, 256, D), bf16), pltpu.SemaphoreType.DMA((2,))],
        name="rows", moved=1 << 20,
    )
    copies, place = lax.optimization_barrier((copies, place))
    gathered = exchange(copies)
    teacher_exp, mass = call(
        teacher_kernel, [resident, rows], gathered, teacher_weight,
        limit=16, name="teacher_exp", flops=product, moved=matrix, exps=K * T,
    )
    masses = over_token_groups(mass)
    student_exp, total, protos_t, rows_t, weight = call(
        student_kernel, [resident, row, shape((D, K), bf16), shape((D, T), bf16), row], gathered, student_weight,
        limit=14, name="student_exp", flops=product, moved=matrix, exps=K * T,
    )
    (copies,) = call(
        first_token_mass_kernel, [shape((GROUPS, PACKED, LANES), f32)], *masses, teacher_exp, student_exp,
        name="token_mass", moved=matrix // 2,
    )
    copies, total = lax.optimization_barrier((copies, total))
    parts = exchange(copies)
    (mass,) = call(
        first_proto_mass_kernel, [rows], parts, teacher_exp, name="proto_mass", moved=matrix // 2
    )
    masses = over_token_groups(mass)
    (student_part,) = call(
        student_unit_kernel, [shape((D, T), f32)], protos_t, student_exp,
        name="student_unit_grads", flops=product, moved=matrix,
    )
    (copies,) = call(
        token_mass_kernel, [shape((GROUPS, 2 * PACKED, LANES), f32)], *masses, teacher_exp, total,
        name="token_mass", moved=matrix // 2,
    )
    copies, student_part = lax.optimization_barrier((copies, student_part))
    parts = exchange(copies)
    mass, total = call(
        proto_mass_kernel, [rows, row], parts, teacher_exp, name="proto_mass", moved=matrix // 2
    )
    masses = over_token_groups(mass)
    (student_proto,) = call(
        student_proto_kernel, [shape((K, D), bf16)], rows_t, total, weight, student_exp,
        name="student_proto_grads", flops=product, moved=matrix,
    )
    copies, proto_scale, teacher_part = call(
        last_token_mass_kernel,
        [shape((GROUPS, 2 * PACKED, LANES), f32), rows, shape((D, T), f32)],
        *masses, teacher_exp, protos_t, rows_t,
        scratch=[pltpu.VMEM((D + 16, K), bf16)], limit=12, name="last_token_mass", flops=product, moved=matrix,
    )
    copies, student_proto = lax.optimization_barrier((copies, student_proto))
    parts = exchange(copies)
    loss, teacher_scale, own, one, two, three = call(
        combine_kernel,
        [shape((8, LANES), f32), row, shape((256, D), f32)] + [shape((256, D), bf16)] * 3,
        place, parts, total, weight, student_part, teacher_part,
        scratch=[pltpu.VMEM((16, T), f32)], name="combine",
    )
    one, two, three = turn(one, "y", 1), turn(two, "y", 2), turn(three, "y", 3)

    def proto_grads(name, chunks, outs):
        return call(
            lambda *refs: proto_kernel(chunks, *refs), outs,
            place, loss, teacher_scale, proto_scale, rows_t, teacher_exp, student_proto,
            name=name,
        )

    keep, send = shape((1024, D), f32), shape((1024, D), bf16)
    (far,) = proto_grads("proto_grads_far_send", [(2, True)], [shape((1040, D), bf16)])
    from_far = flip(far, "c")
    next_send, last_send, far_keep = proto_grads(
        "proto_grads_far", [(1, True), (3, True), (2, False)], [send, send, keep]
    )
    from_next, from_last = flip(next_send, "c"), flip(last_send, "c")
    piece, half = shape((272, D), bf16), shape((512, D), bf16)
    up, up2, down, down2, loss = call(
        first_fold_kernel, [piece, shape((256, D), bf16)] * 2 + [shape((8, LANES), f32)],
        far_keep, from_far, loss, name="first_fold",
    )
    up, up2, down, down2 = turn(up, "z", 1), turn(up2, "z", 1), turn(down, "z", 3), turn(down2, "z", 3)
    near_send, next_keep, last_keep, near_keep = proto_grads(
        "proto_grads_near", [(0, True), (1, False), (3, False), (0, False)], [send, keep, keep, keep]
    )
    from_near = flip(near_send, "c")
    own, one, two, three = call(
        fold_rows_kernel, [shape((64, D), f32)] + [shape((64, D), bf16)] * 3,
        place, own, one, two, three, name="fold_rows",
    )
    one, two, three = turn(one, "x", 1), turn(two, "x", 2), turn(three, "x", 3)
    first, second, third, fourth = call(
        second_fold_kernel, [shape((528, D), bf16), half, half, half],
        next_keep, from_next, last_keep, from_last, up, up2, down, down2, name="second_fold",
    )
    first, second, third, fourth = turn(first, "z", 1), turn(second, "z", 1), turn(third, "z", 3), turn(fourth, "z", 3)
    (feature_grads,) = call(
        feature_grads_kernel, [shape((64, D), f32)], student_rows, own, one, two, three, name="feature_grads",
    )
    weight_grads, loss = call(
        weight_grads_kernel, [keep, shape((1, 1), f32)],
        place, student_weight, near_keep, from_near, loss, up, down, first, second, third, fourth, far=(1,),
        scratch=[pltpu.VMEM((1024, D), bf16), pltpu.SemaphoreType.DMA], name="weight_grads",
    )
    return loss.reshape(()), feature_grads.reshape(2, 32, D), weight_grads


def solution(mesh):
    fine = Mesh(mesh.devices.reshape(4, 2, 4, 4), ("z", "c", "y", "x"))
    every, proto = ("z", "c", "y", "x"), ("y", "x")
    return jax.shard_map(
        local,
        mesh=fine,
        in_specs=(
            P(every, None, None),
            P(every, None, None),
            P(every, None),
            P(every, None),
            P(proto, None),
            P(proto, None),
        ),
        out_specs=(P(), P(every, None, None), P(("y", "x", "z", "c"), None)),
        check_vma=False,
    )
```

```python
import jax
import jax.numpy as jnp
from jax import lax
from jax.experimental import pallas as pl
from jax.experimental.pallas import tpu as pltpu
from jax.sharding import Mesh, PartitionSpec as P

teacher_temp = 0.07
student_temp = 0.1
epsilon = 1e-06
LOG2E = 1.4426950408889634
SWEEPS = 3
TOKENS = 8192
T, K, D = 1024, 8192, 256
BLOCK = 512
LANES = 128
f32, bf16 = jnp.float32, jnp.bfloat16
GROUPS = 16
PACKED = T // LANES
SAME_TOKENS = ("y", "x")
VMEM = pl.BlockSpec(memory_space=pltpu.VMEM)
SMEM = pl.BlockSpec(memory_space=pltpu.SMEM)


def nt(left, right):
    return lax.dot_general(left, right, (((1,), (1,)), ((), ())), preferred_element_type=f32)


def nn(left, right):
    return lax.dot_general(left, right, (((1,), (0,)), ((), ())), preferred_element_type=f32)


def normalize_rows(values):
    scale = lax.rsqrt(jnp.sum(values * values, axis=-1, keepdims=True) + epsilon)
    return values * scale, scale


def three_rows(row):
    high = row.astype(bf16).astype(f32)
    rest = row - high
    middle = rest.astype(bf16).astype(f32)
    low = rest - middle
    index = lax.broadcasted_iota(jnp.int32, (16, row.shape[1]), 0)
    picked = jnp.where(index == 0, high, jnp.where(index == 1, middle, jnp.where(index == 2, low, 0.0)))
    return picked.astype(bf16)


def as_row(packed):
    return jnp.concatenate([packed[j : j + 1, :] for j in range(packed.shape[0])], axis=1)


def store_packed(ref, start, row):
    for j in range(row.shape[1] // LANES):
        ref[start + j : start + j + 1, :] = row[:, j * LANES : (j + 1) * LANES]


def call(kernel, outs, *args, far=(), scratch=(), limit=11, name=None, flops=0, moved=0, exps=0):
    specs = [SMEM if arg.dtype == jnp.int32 and arg.ndim == 1 else VMEM for arg in args]
    args = list(args)
    for i in far:
        specs[i] = pl.BlockSpec(memory_space=pl.ANY)
        args[i] = pltpu.with_memory_space_constraint(args[i], pltpu.HBM)
    return pl.pallas_call(
        kernel,
        out_shape=outs,
        in_specs=specs,
        out_specs=[VMEM] * len(outs),
        scratch_shapes=list(scratch),
        compiler_params=pltpu.CompilerParams(vmem_limit_bytes=limit << 20),
        cost_estimate=pl.CostEstimate(flops=flops, bytes_accessed=moved, transcendentals=exps),
        name=name,
    )(*args)


def lane_sums(values):
    part = values[:, 0:LANES]
    for j in range(1, values.shape[1] // LANES):
        part = part + values[:, j * LANES : (j + 1) * LANES]
    return jnp.sum(jnp.transpose(part), axis=0, keepdims=True)


def pick_rows(patches_ref, positions_ref, image):
    patch = lax.broadcasted_iota(jnp.int32, (256, 32), 0)
    chosen = (patch == positions_ref[image : image + 1, :]).astype(f32).astype(bf16)
    return lax.dot_general(chosen, patches_ref[image], (((0,), (0,)), ((), ())), preferred_element_type=f32)


def rows_kernel(
    far_teacher_ref, far_student_ref, far_positions_ref, far_weight_ref, unit_ref, rows_ref,
    teacher_ref, student_ref, positions_ref, weight_ref, arrived
):
    pairs = (
        (far_positions_ref, positions_ref), (far_teacher_ref, teacher_ref),
        (far_student_ref, student_ref), (far_weight_ref, weight_ref),
    )
    reads = [pltpu.make_async_copy(far, near, arrived.at[i]) for i, (far, near) in enumerate(pairs)]
    for read in reads:
        read.start()
    reads[0].wait()
    reads[1].wait()
    for image in range(2):
        here = slice(image * 32, (image + 1) * 32)
        unit_ref[here, :] = normalize_rows(pick_rows(teacher_ref, positions_ref, image))[0].astype(bf16)
    reads[2].wait()
    for image in range(2):
        here = slice(image * 32, (image + 1) * 32)
        rows = pick_rows(student_ref, positions_ref, image)
        rows_ref[here, :] = rows
        unit_ref[64 + image * 32 : 96 + image * 32, :] = normalize_rows(rows)[0].astype(bf16)
    reads[3].wait()
    row = lax.broadcasted_iota(jnp.int32, (16, 32), 0)
    weight = weight_ref[...].astype(f32)
    weight = jnp.where(row == 0, weight[0:1], jnp.where(row == 1, weight[1:2], 0.0)).astype(bf16)
    same = lax.broadcasted_iota(jnp.int32, (32, D), 0) == lax.broadcasted_iota(jnp.int32, (32, D), 1)
    unit_ref[128:144, :] = nn(weight, same.astype(f32).astype(bf16)).astype(bf16)


def source(place_ref, y_step, x_step):
    return lax.rem(place_ref[2] + 4 - y_step, 4) * 4 + lax.rem(place_ref[3] + 4 - x_step, 4)


def fetch(far_ref, near_ref, arrived):
    reads = [
        pltpu.make_async_copy(
            far_ref.at[pl.ds(b * BLOCK, BLOCK), :], near_ref.at[pl.ds(b * BLOCK, BLOCK), :], arrived.at[b]
        )
        for b in range(K // BLOCK)
    ]
    for read in reads:
        read.start()
    return reads


def protos_kernel(far_weight_ref, out_ref, weight_ref, arrived):
    for b, read in enumerate(fetch(far_weight_ref, weight_ref, arrived)):
        here = slice(b * BLOCK, (b + 1) * BLOCK)
        read.wait()
        out_ref[here, :] = normalize_rows(weight_ref[here, :].astype(f32))[0].astype(bf16)


def protos_t_kernel(far_weight_ref, out_ref, out_t_ref, weight_ref, arrived):
    for b, read in enumerate(fetch(far_weight_ref, weight_ref, arrived)):
        here = slice(b * BLOCK, (b + 1) * BLOCK)
        read.wait()
        protos = normalize_rows(weight_ref[here, :].astype(f32))[0].astype(bf16)
        out_ref[here, :] = protos
        out_t_ref[:, here] = jnp.transpose(protos.astype(f32)).astype(bf16)


def teacher_kernel(place_ref, a_ref, b_ref, c_ref, d_ref, protos_ref, exp_ref, mass_ref, rows_ref):
    for x_step, ref in enumerate((a_ref, b_ref, c_ref, d_ref)):
        for y_step in range(4):
            start = pl.multiple_of(source(place_ref, y_step, x_step) * 64, 64)
            rows_ref[pl.ds(start, 64), :] = ref[y_step * 144 : y_step * 144 + 64, :]
    rows = rows_ref[...]
    for b in range(K // BLOCK):
        here = slice(b * BLOCK, (b + 1) * BLOCK)
        values = jnp.exp2(nt(protos_ref[here, :], rows) * (LOG2E / teacher_temp))
        exp_ref[here, :] = values.astype(bf16)
        store_packed(mass_ref, b * BLOCK // LANES, lane_sums(values))


def student_kernel(
    place_ref, a_ref, b_ref, c_ref, d_ref, protos_ref, protos_t_ref,
    total_ref, rows_ref, rows_t_ref, token_weight_ref, grads_ref, extra_ref
):
    for x_step, ref in enumerate((a_ref, b_ref, c_ref, d_ref)):
        for y_step in range(4):
            place = source(place_ref, y_step, x_step)
            rows_ref[pl.ds(pl.multiple_of(place * 64, 64), 64), :] = ref[y_step * 144 + 64 : y_step * 144 + 128, :]
            extra_ref[pl.ds(place, 1)] = ref[y_step * 144 + 128 : y_step * 144 + 144, 0:LANES].astype(f32)[None]
    rows = rows_ref[...]
    rows_t_ref[...] = jnp.transpose(rows.astype(f32)).astype(bf16)
    for j in range(PACKED):
        row = jnp.zeros((1, LANES), f32)
        for piece in range(4):
            row = row + pltpu.roll(extra_ref[2 * j + piece // 2], piece * 32, 1)[piece % 2 : piece % 2 + 1]
        token_weight_ref[j : j + 1, :] = row
    grads_ref[...] = jnp.zeros_like(grads_ref)

    def step(b, total):
        here = pl.ds(pl.multiple_of(b * BLOCK, BLOCK), BLOCK)
        values = jnp.exp2(nt(protos_ref[here, :], rows) * (LOG2E / student_temp))
        grads_ref[...] += nn(protos_t_ref[:, here], values.astype(bf16))
        return total + jnp.sum(values.reshape(BLOCK // 8, 8, T), axis=0)

    total = lax.fori_loop(0, K // BLOCK, step, jnp.zeros((8, T), f32), unroll=4)
    store_packed(total_ref, 0, jnp.sum(total, axis=0, keepdims=True))


def student_proto_kernel(protos_ref, rows_ref, rows_t_ref, total_ref, weight_ref, out_ref):
    rows = rows_ref[...]
    scale = as_row(weight_ref[...] / (student_temp * total_ref[...]))
    right = (rows_t_ref[...].astype(f32) * scale).astype(bf16)

    def step(b, carry):
        here = pl.ds(pl.multiple_of(b * BLOCK, BLOCK), BLOCK)
        values = jnp.exp2(nt(protos_ref[here, :], rows) * (LOG2E / student_temp))
        out_ref[here, :] = nt(values.astype(bf16), right).astype(bf16)
        return carry

    lax.fori_loop(0, K // BLOCK, step, 0, unroll=4)


def store_copies(ref, start, row):
    for j in range(row.shape[1] // LANES):
        piece = row[:, j * LANES : (j + 1) * LANES]
        for copy in range(GROUPS):
            ref[copy, start + j : start + j + 1, :] = piece


def token_mass(packed, exp_ref, mass_ref):
    scale = three_rows(as_row(packed))
    total = jnp.zeros((16, T), f32)
    for b in range(K // BLOCK):
        here = slice(b * BLOCK, (b + 1) * BLOCK)
        total = total + nn(scale[:, here], exp_ref[here, :])
    store_copies(mass_ref, 0, jnp.sum(total, axis=0, keepdims=True))


def first_token_mass_kernel(near_ref, far_ref, exp_ref, mass_ref):
    token_mass(1.0 / (near_ref[...] + far_ref[...]), exp_ref, mass_ref)


def token_mass_kernel(near_ref, far_ref, exp_ref, student_ref, mass_ref):
    token_mass(1.0 / (near_ref[...] + far_ref[...]), exp_ref, mass_ref)
    student = student_ref[...]
    for copy in range(GROUPS):
        mass_ref[copy, PACKED : 2 * PACKED, :] = student


def last_token_mass_kernel(
    near_ref, far_ref, exp_ref, protos_t_ref, rows_t_ref, mass_ref, scale_ref, grads_ref, left_ref
):
    packed = 1.0 / (near_ref[...] + far_ref[...])
    scale_ref[...] = packed
    scale = as_row(packed)
    left_ref[D : D + 16, :] = three_rows(scale)
    left_ref[0:D, :] = (protos_t_ref[...].astype(f32) * scale).astype(bf16)
    for j in range(T // BLOCK):
        here = slice(j * BLOCK, (j + 1) * BLOCK)
        both = nn(left_ref[...], exp_ref[:, here])
        grads = both[0:D]
        grads_ref[:, here] = grads
        store_copies(mass_ref, j * BLOCK // LANES, jnp.sum(both[D:], axis=0, keepdims=True))
        cross = jnp.sum(grads * rows_t_ref[:, here].astype(f32), axis=0, keepdims=True)
        store_copies(mass_ref, (T + j * BLOCK) // LANES, cross)


def column_mass(scale, exp_ref, mass_ref):
    split = three_rows(scale)
    for b in range(K // 1024):
        start = b * 1024 + 640
        row = jnp.sum(nt(split, exp_ref[start : start + 384, :]), axis=0, keepdims=True)
        store_packed(mass_ref, start // LANES, row)
        start = b * 1024
        part = jnp.zeros((640, LANES), f32)
        for j in range(T // LANES):
            lanes = slice(j * LANES, (j + 1) * LANES)
            part = part + exp_ref[start : start + 640, lanes].astype(f32) * scale[:, lanes]
        store_packed(mass_ref, start // LANES, jnp.sum(jnp.transpose(part), axis=0, keepdims=True))


def first_proto_mass_kernel(parts_ref, exp_ref, mass_ref):
    column_mass(1.0 / as_row(jnp.sum(parts_ref[...], axis=0)), exp_ref, mass_ref)


def proto_mass_kernel(parts_ref, exp_ref, mass_ref, total_ref):
    parts = jnp.sum(parts_ref[...], axis=0)
    total_ref[...] = parts[PACKED:]
    column_mass(1.0 / as_row(parts[0:PACKED]), exp_ref, mass_ref)


def combine_kernel(
    place_ref, parts_ref, total_ref, weight_ref, student_ref, teacher_ref,
    loss_ref, scale_ref, keep_ref, one_ref, two_ref, three_ref, rows_ref
):
    parts = jnp.sum(parts_ref[...], axis=0)
    token_scale = 1.0 / parts[0:PACKED]
    total, weight = total_ref[...], weight_ref[...]
    cross = jnp.log(total) - token_scale * parts[PACKED:] / student_temp
    loss_ref[...] = jnp.full((8, LANES), jnp.sum(weight * cross) / TOKENS, f32)
    teacher_scale = weight * token_scale / student_temp
    scale_ref[...] = teacher_scale
    rows_ref[0:1, :] = as_row(weight / (student_temp * total))
    rows_ref[8:9, :] = as_row(teacher_scale)
    for step, ref in enumerate((keep_ref, one_ref, two_ref, three_ref)):
        block = lax.rem(place_ref[2] + step, 4)
        here = pl.ds(pl.multiple_of(block * 256, 256), 256)
        grads = student_ref[:, here] * rows_ref[0:1, here] - teacher_ref[:, here] * rows_ref[8:9, here]
        ref[...] = jnp.transpose(grads).astype(ref.dtype)


def fold_rows_kernel(place_ref, own_ref, a_ref, b_ref, c_ref, keep_ref, one_ref, two_ref, three_ref):
    for step, ref in enumerate((keep_ref, one_ref, two_ref, three_ref)):
        block = lax.rem(place_ref[3] + step, 4)
        here = pl.ds(pl.multiple_of(block * 64, 64), 64)
        total = own_ref[here, :] + a_ref[here, :].astype(f32) + b_ref[here, :].astype(f32)
        ref[...] = (total + c_ref[here, :].astype(f32)).astype(ref.dtype)


def proto_kernel(chunks, place_ref, loss_ref, teacher_scale_ref, scale_ref, rows_t_ref, exp_ref, student_ref, *outs):
    right = (rows_t_ref[...].astype(f32) * as_row(teacher_scale_ref[...])).astype(bf16)
    places = [(ref, i * 1024) for ref in outs for i in range(ref.shape[0] // 1024)]
    for (z_step, core_flip), (ref, first) in zip(chunks, places):
        z = lax.rem(place_ref[0] + z_step, 4)
        core = 1 - place_ref[1] if core_flip else place_ref[1]
        chunk = z * 2 + core
        if ref.shape[0] == 1040:
            ref[1024:1040, :] = loss_rows(loss_ref[0:1, :])
        for b in range(2):
            start = pl.multiple_of(chunk * 1024 + b * 512, 512)
            product = nt(exp_ref[pl.ds(start, 512), :], right)
            student = student_ref[pl.ds(start, 512), :].astype(f32)
            for j in range(4):
                row = scale_ref[pl.ds(chunk * 8 + b * 4 + j, 1), :]
                column = jnp.transpose(jnp.broadcast_to(row, (LANES, LANES)))
                column = jnp.concatenate([column, column], axis=1)
                here = slice(j * LANES, (j + 1) * LANES)
                value = student[here] - product[here] * column
                to = first + b * 512 + j * LANES
                ref[to : to + LANES, :] = value.astype(ref.dtype)


def loss_rows(row):
    return three_rows(jnp.concatenate([row, row], axis=1))


def loss_of(rows):
    return jnp.sum(rows.astype(f32), axis=0, keepdims=True)[:, 0:LANES]


def first_fold_kernel(own_ref, core_ref, loss_ref, up_ref, down_ref, loss_out_ref):
    loss = loss_ref[0:1, :] + loss_of(core_ref[1024:1040, :])
    loss_out_ref[...] = jnp.broadcast_to(loss, (8, LANES))
    for i, ref in enumerate((up_ref, down_ref)):
        here = slice(i * 512, (i + 1) * 512)
        ref[0:512, :] = (own_ref[here, :] + core_ref[here, :].astype(f32)).astype(bf16)
        ref[512:528, :] = loss_rows(loss)


def second_fold_kernel(own_ref, core_ref, up_ref, down_ref, next_ref, last_ref):
    for i in range(4):
        here = slice(i * 512, (i + 1) * 512)
        value = own_ref[here, :] + core_ref[here, :].astype(f32)
        if i in (0, 3):
            value = value + (up_ref if i == 0 else down_ref)[0:512, :].astype(f32)
        to = i % 2 * 512
        (next_ref if i < 2 else last_ref)[to : to + 512, :] = value.astype(bf16)
    next_ref[1024:1040, :] = up_ref[512:528, :]
    last_ref[1024:1040, :] = up_ref[512:528, :]


def normalize_back(unit, scale, grad):
    return scale * (grad - unit * jnp.sum(unit * grad, axis=-1, keepdims=True))


def own_kernel(place_ref, far_weight_ref, own_ref, core_ref, unit_ref, scale_ref, base_ref, weight_ref, arrived):
    start = pl.multiple_of((place_ref[0] * 2 + place_ref[1]) * 1024, 1024)
    read = pltpu.make_async_copy(far_weight_ref.at[pl.ds(start, 1024), :], weight_ref, arrived)
    read.start()
    base_ref[...] = own_ref[2048:3072, :] + core_ref[2048:3072, :].astype(f32)
    read.wait()
    unit, scale = normalize_rows(weight_ref[...].astype(f32))
    unit_ref[...] = unit
    scale_ref[...] = jnp.broadcast_to(scale, (1024, LANES))


def weight_grads_kernel(
    unit_ref, scale_ref, base_ref, loss_ref, up_ref, down_ref, last_ref, next_ref, out_ref, loss_out_ref
):
    far = loss_ref[0:1, :] + loss_of(last_ref[1024:1040, :])
    loss = far + (loss_of(up_ref[512:528, :]) + loss_of(down_ref[512:528, :]))
    loss_out_ref[...] = loss[:, 0:1]
    grads = base_ref[...] + (last_ref[0:1024, :].astype(f32) + next_ref[0:1024, :].astype(f32))
    out_ref[...] = normalize_back(unit_ref[...], scale_ref[:, 0:1], grads)


def feature_grads_kernel(rows_ref, own_ref, a_ref, b_ref, c_ref, out_ref):
    grads = own_ref[...] + a_ref[...].astype(f32) + b_ref[...].astype(f32) + c_ref[...].astype(f32)
    unit, scale = normalize_rows(rows_ref[...])
    out_ref[...] = normalize_back(unit, scale, grads)


def turn(values, axis, step):
    return lax.ppermute(values, axis, [(i, (i + step) % 4) for i in range(4)])


def flip(values, axis):
    return lax.ppermute(values, axis, [(0, 1), (1, 0)])


def over_token_groups(values):
    pairs = [(i, i ^ 1) for i in range(4)]
    both = [(z * 2 + c, (z ^ 1) * 2 + (1 - c)) for z in range(4) for c in range(2)]
    near = (values + flip(values, "c")) + (lax.ppermute(values, "z", pairs) + lax.ppermute(values, ("z", "c"), both))
    return near, lax.ppermute(near, "z", [(i, 3 - i) for i in range(4)])


def exchange(blocks):
    return lax.all_to_all(blocks, SAME_TOKENS, 0, 0, tiled=True)


def local(student_patches, teacher_patches, mask_positions, token_weight, student_weight, teacher_weight):
    z, c, y, x = (lax.axis_index(name) for name in ("z", "c", "y", "x"))
    place = jnp.stack([z, c, y, x]).astype(jnp.int32)
    matrix = K * T * 2
    product = 2 * K * T * D
    shape = jax.ShapeDtypeStruct
    row, rows = shape((PACKED, LANES), f32), shape((K // LANES, LANES), f32)
    resident = pltpu.VMEM((K, T), bf16)

    DMA = pltpu.SemaphoreType.DMA
    unit_rows, student_rows = call(
        rows_kernel, [shape((144, D), bf16), shape((64, D), f32)],
        teacher_patches, student_patches, mask_positions, token_weight, far=(0, 1, 2, 3),
        scratch=[
            pltpu.VMEM((2, 256, D), bf16), pltpu.VMEM((2, 256, D), bf16),
            pltpu.VMEM((2, 32), jnp.int32), pltpu.VMEM((2, 32), bf16), DMA((4,)),
        ],
        name="rows",
    )
    unit_rows, place = lax.optimization_barrier((unit_rows, place))
    parts = [unit_rows] + [turn(unit_rows, "y", i) for i in (1, 2, 3)]
    protos = pltpu.VMEM((K, D), bf16)
    loading = dict(far=(0,), scratch=[protos, DMA((K // BLOCK,))])
    (teacher_protos,) = call(protos_kernel, [protos], teacher_weight, name="teacher_protos", moved=2 * K * D, **loading)
    *parts, teacher_protos = lax.optimization_barrier((*parts, teacher_protos))
    column = jnp.concatenate(parts, axis=0)
    gathered = [column] + [turn(column, "x", i) for i in (1, 2, 3)]
    student_protos, protos_t = call(
        protos_t_kernel, [shape((K, D), bf16), shape((D, K), bf16)], student_weight,
        name="student_protos", moved=2 * K * D, **loading,
    )
    *gathered, student_protos = lax.optimization_barrier((*gathered, student_protos))
    teacher_exp, mass = call(
        teacher_kernel, [resident, rows], place, *gathered, teacher_protos,
        scratch=[pltpu.VMEM((T, D), bf16)], limit=16, name="teacher_exp",
    )
    masses = over_token_groups(mass)
    total, student_all, rows_t, weight, student_part = call(
        student_kernel,
        [row, shape((T, D), bf16), shape((D, T), bf16), row, shape((D, T), f32)],
        place, *gathered, student_protos, protos_t,
        scratch=[pltpu.VMEM((GROUPS, 16, LANES), f32)],
        limit=16, name="student_unit_grads", flops=2 * product, moved=matrix, exps=K * T,
    )
    (copies,) = call(
        first_token_mass_kernel, [shape((GROUPS, PACKED, LANES), f32)], *masses, teacher_exp,
        name="token_mass", moved=matrix // 2,
    )
    copies, total, student_part = lax.optimization_barrier((copies, total, student_part))
    parts = exchange(copies)
    (mass,) = call(
        first_proto_mass_kernel, [rows], parts, teacher_exp, name="proto_mass", moved=matrix // 2
    )
    masses = over_token_groups(mass)
    (copies,) = call(
        token_mass_kernel, [shape((GROUPS, 2 * PACKED, LANES), f32)], *masses, teacher_exp, total,
        name="token_mass", moved=matrix // 2,
    )
    parts = exchange(copies)
    mass, total = call(
        proto_mass_kernel, [rows, row], parts, teacher_exp, name="proto_mass", moved=matrix // 2
    )
    masses = over_token_groups(mass)
    (student_proto,) = call(
        student_proto_kernel, [shape((K, D), bf16)], student_protos, student_all, rows_t, total, weight,
        limit=16, name="student_proto_grads", flops=2 * product, moved=matrix, exps=K * T,
    )
    copies, proto_scale, teacher_part = call(
        last_token_mass_kernel,
        [shape((GROUPS, 2 * PACKED, LANES), f32), rows, shape((D, T), f32)],
        *masses, teacher_exp, protos_t, rows_t,
        scratch=[pltpu.VMEM((D + 16, K), bf16)], limit=12, name="last_token_mass", flops=product, moved=matrix,
    )
    copies, student_proto = lax.optimization_barrier((copies, student_proto))
    parts = exchange(copies)
    loss, teacher_scale, own, one, two, three = call(
        combine_kernel,
        [shape((8, LANES), f32), row, shape((256, D), f32)] + [shape((256, D), bf16)] * 3,
        place, parts, total, weight, student_part, teacher_part,
        scratch=[pltpu.VMEM((16, T), f32)], name="combine",
    )
    one, two, three = turn(one, "y", 1), turn(two, "y", 2), turn(three, "y", 3)

    def proto_grads(name, chunks, outs):
        return call(
            lambda *refs: proto_kernel(chunks, *refs), outs,
            place, loss, teacher_scale, proto_scale, rows_t, teacher_exp, student_proto,
            name=name,
        )

    keep = shape((1024, D), f32)
    (far,) = proto_grads("proto_grads_far_send", [(2, True)], [shape((1040, D), bf16)])
    from_far = flip(far, "c")
    teacher_scale, far = lax.optimization_barrier((teacher_scale, far))
    (far_keep,) = proto_grads("proto_grads_far_keep", [(2, False)], [keep])
    (others,) = proto_grads("proto_grads_send", [(1, True), (3, True), (0, True)], [shape((3072, D), bf16)])
    from_others = flip(others, "c")
    far_keep, others, one, two, three = lax.optimization_barrier((far_keep, others, one, two, three))
    piece, side = shape((528, D), bf16), shape((1040, D), bf16)
    up, down, loss_here = call(
        first_fold_kernel, [piece, piece, shape((8, LANES), f32)], far_keep, from_far, loss, name="first_fold",
    )
    up_there, down_there = turn(up, "z", 1), turn(down, "z", 3)
    teacher_scale, loss_here = lax.optimization_barrier((teacher_scale, loss_here))
    (others_keep,) = proto_grads("proto_grads_keep", [(1, False), (3, False), (0, False)], [shape((3072, D), f32)])
    own, others_keep = lax.optimization_barrier((own, others_keep))
    own, one, two, three = call(
        fold_rows_kernel, [shape((64, D), f32)] + [shape((64, D), bf16)] * 3,
        place, own, one, two, three, name="fold_rows",
    )
    first, second = call(
        second_fold_kernel, [side, side], others_keep, from_others, up_there, down_there, name="second_fold",
    )
    own, first = lax.optimization_barrier((own, first))
    one, two, three = turn(one, "x", 1), turn(two, "x", 2), turn(three, "x", 3)
    from_last, from_next = turn(first, "z", 1), turn(second, "z", 3)
    unit, scale, base = call(
        own_kernel, [keep, shape((1024, LANES), f32), keep], place, student_weight, others_keep, from_others, far=(1,),
        scratch=[pltpu.VMEM((1024, D), bf16), DMA], name="own",
    )
    (feature_grads,) = call(
        feature_grads_kernel, [shape((64, D), f32)], student_rows, own, one, two, three, name="feature_grads",
    )
    weight_grads, loss = call(
        weight_grads_kernel, [keep, shape((1, 1), f32)],
        unit, scale, base, loss_here, up_there, down_there, from_last, from_next, name="weight_grads",
    )
    return loss.reshape(()), feature_grads.reshape(2, 32, D), weight_grads


def solution(mesh):
    fine = Mesh(mesh.devices.reshape(4, 2, 4, 4), ("z", "c", "y", "x"))
    every, proto = ("z", "c", "y", "x"), ("y", "x")
    return jax.shard_map(
        local,
        mesh=fine,
        in_specs=(
            P(every, None, None),
            P(every, None, None),
            P(every, None),
            P(every, None),
            P(proto, None),
            P(proto, None),
        ),
        out_specs=(P(), P(every, None, None), P(("y", "x", "z", "c"), None)),
        check_vma=False,
    )
```

```python
import jax
import jax.numpy as jnp
from jax import lax
from jax.experimental import pallas as pl
from jax.experimental.pallas import tpu as pltpu
from jax.sharding import Mesh, PartitionSpec as P

teacher_temp = 0.07
student_temp = 0.1
epsilon = 1e-06
LOG2E = 1.4426950408889634
SWEEPS = 3
TOKENS = 8192
T, K, D = 1024, 8192, 256
BLOCK = 512
LANES = 128
f32, bf16 = jnp.float32, jnp.bfloat16
GROUPS = 16
PACKED = T // LANES
SAME_TOKENS = ("y", "x")
VMEM = pl.BlockSpec(memory_space=pltpu.VMEM)
SMEM = pl.BlockSpec(memory_space=pltpu.SMEM)


def nt(left, right):
    return lax.dot_general(left, right, (((1,), (1,)), ((), ())), preferred_element_type=f32)


def nn(left, right):
    return lax.dot_general(left, right, (((1,), (0,)), ((), ())), preferred_element_type=f32)


def normalize_rows(values):
    scale = lax.rsqrt(jnp.sum(values * values, axis=-1, keepdims=True) + epsilon)
    return values * scale, scale


def three_rows(row):
    high = row.astype(bf16).astype(f32)
    rest = row - high
    middle = rest.astype(bf16).astype(f32)
    low = rest - middle
    index = lax.broadcasted_iota(jnp.int32, (16, row.shape[1]), 0)
    picked = jnp.where(index == 0, high, jnp.where(index == 1, middle, jnp.where(index == 2, low, 0.0)))
    return picked.astype(bf16)


def as_row(packed):
    return jnp.concatenate([packed[j : j + 1, :] for j in range(packed.shape[0])], axis=1)


def store_packed(ref, start, row):
    for j in range(row.shape[1] // LANES):
        ref[start + j : start + j + 1, :] = row[:, j * LANES : (j + 1) * LANES]


def call(kernel, outs, *args, far=(), scratch=(), limit=11, name=None, flops=0, moved=0, exps=0):
    specs = [SMEM if arg.dtype == jnp.int32 and arg.ndim == 1 else VMEM for arg in args]
    args = list(args)
    for i in far:
        specs[i] = pl.BlockSpec(memory_space=pl.ANY)
        args[i] = pltpu.with_memory_space_constraint(args[i], pltpu.HBM)
    return pl.pallas_call(
        kernel,
        out_shape=outs,
        in_specs=specs,
        out_specs=[VMEM] * len(outs),
        scratch_shapes=list(scratch),
        compiler_params=pltpu.CompilerParams(vmem_limit_bytes=limit << 20),
        cost_estimate=pl.CostEstimate(flops=flops, bytes_accessed=moved, transcendentals=exps),
        name=name,
    )(*args)


def lane_sums(values):
    part = values[:, 0:LANES]
    for j in range(1, values.shape[1] // LANES):
        part = part + values[:, j * LANES : (j + 1) * LANES]
    return jnp.sum(jnp.transpose(part), axis=0, keepdims=True)


def pick_rows(patches_ref, positions_ref, image):
    patch = lax.broadcasted_iota(jnp.int32, (256, 32), 0)
    chosen = (patch == positions_ref[image : image + 1, :]).astype(f32).astype(bf16)
    return lax.dot_general(chosen, patches_ref[image], (((0,), (0,)), ((), ())), preferred_element_type=f32)


def rows_kernel(
    far_teacher_ref, far_student_ref, far_positions_ref, far_weight_ref, unit_ref, rows_ref,
    teacher_ref, student_ref, positions_ref, weight_ref, arrived
):
    pairs = (
        (far_positions_ref, positions_ref), (far_teacher_ref, teacher_ref),
        (far_student_ref, student_ref), (far_weight_ref, weight_ref),
    )
    reads = [pltpu.make_async_copy(far, near, arrived.at[i]) for i, (far, near) in enumerate(pairs)]
    for read in reads:
        read.start()
    reads[0].wait()
    reads[1].wait()
    for image in range(2):
        here = slice(image * 32, (image + 1) * 32)
        unit_ref[here, :] = normalize_rows(pick_rows(teacher_ref, positions_ref, image))[0].astype(bf16)
    reads[2].wait()
    for image in range(2):
        here = slice(image * 32, (image + 1) * 32)
        rows = pick_rows(student_ref, positions_ref, image)
        rows_ref[here, :] = rows
        unit_ref[64 + image * 32 : 96 + image * 32, :] = normalize_rows(rows)[0].astype(bf16)
    reads[3].wait()
    row = lax.broadcasted_iota(jnp.int32, (16, 32), 0)
    weight = weight_ref[...].astype(f32)
    weight = jnp.where(row == 0, weight[0:1], jnp.where(row == 1, weight[1:2], 0.0)).astype(bf16)
    same = lax.broadcasted_iota(jnp.int32, (32, D), 0) == lax.broadcasted_iota(jnp.int32, (32, D), 1)
    unit_ref[128:144, :] = nn(weight, same.astype(f32).astype(bf16)).astype(bf16)


def source(place_ref, y_step, x_step):
    return lax.rem(place_ref[2] + 4 - y_step, 4) * 4 + lax.rem(place_ref[3] + 4 - x_step, 4)


def fetch(far_ref, near_ref, arrived):
    reads = [
        pltpu.make_async_copy(
            far_ref.at[pl.ds(b * BLOCK, BLOCK), :], near_ref.at[pl.ds(b * BLOCK, BLOCK), :], arrived.at[b]
        )
        for b in range(K // BLOCK)
    ]
    for read in reads:
        read.start()
    return reads


def protos_kernel(far_weight_ref, out_ref, weight_ref, arrived):
    for b, read in enumerate(fetch(far_weight_ref, weight_ref, arrived)):
        here = slice(b * BLOCK, (b + 1) * BLOCK)
        read.wait()
        out_ref[here, :] = normalize_rows(weight_ref[here, :].astype(f32))[0].astype(bf16)


def protos_t_kernel(far_weight_ref, out_ref, out_t_ref, weight_ref, arrived):
    for b, read in enumerate(fetch(far_weight_ref, weight_ref, arrived)):
        here = slice(b * BLOCK, (b + 1) * BLOCK)
        read.wait()
        protos = normalize_rows(weight_ref[here, :].astype(f32))[0].astype(bf16)
        out_ref[here, :] = protos
        out_t_ref[:, here] = jnp.transpose(protos.astype(f32)).astype(bf16)


def gathered_blocks(place_ref, a_ref, b_ref, c_ref, c2_ref, d_ref):
    for x_step, refs in enumerate(((a_ref,), (b_ref,), (c_ref, c2_ref), (d_ref,))):
        for y_step in range(4):
            ref, at = refs[y_step * len(refs) // 4], y_step % (4 // len(refs)) * 144
            yield source(place_ref, y_step, x_step), ref, at


def teacher_kernel(place_ref, a_ref, b_ref, c_ref, c2_ref, d_ref, protos_ref, exp_ref, mass_ref, rows_ref):
    for place, ref, at in gathered_blocks(place_ref, a_ref, b_ref, c_ref, c2_ref, d_ref):
        rows_ref[pl.ds(pl.multiple_of(place * 64, 64), 64), :] = ref[at : at + 64, :]
    rows = rows_ref[...]
    for b in range(K // BLOCK):
        here = slice(b * BLOCK, (b + 1) * BLOCK)
        values = jnp.exp2(nt(protos_ref[here, :], rows) * (LOG2E / teacher_temp))
        exp_ref[here, :] = values.astype(bf16)
        store_packed(mass_ref, b * BLOCK // LANES, lane_sums(values))


def student_kernel(
    place_ref, a_ref, b_ref, c_ref, c2_ref, d_ref, protos_ref, protos_t_ref,
    total_ref, rows_ref, rows_t_ref, token_weight_ref, grads_ref, extra_ref
):
    for place, ref, at in gathered_blocks(place_ref, a_ref, b_ref, c_ref, c2_ref, d_ref):
        rows_ref[pl.ds(pl.multiple_of(place * 64, 64), 64), :] = ref[at + 64 : at + 128, :]
        extra_ref[pl.ds(place, 1)] = ref[at + 128 : at + 144, 0:LANES].astype(f32)[None]
    rows = rows_ref[...]
    rows_t_ref[...] = jnp.transpose(rows.astype(f32)).astype(bf16)
    for j in range(PACKED):
        row = jnp.zeros((1, LANES), f32)
        for piece in range(4):
            row = row + pltpu.roll(extra_ref[2 * j + piece // 2], piece * 32, 1)[piece % 2 : piece % 2 + 1]
        token_weight_ref[j : j + 1, :] = row
    grads_ref[...] = jnp.zeros_like(grads_ref)

    def step(b, total):
        here = pl.ds(pl.multiple_of(b * BLOCK, BLOCK), BLOCK)
        values = jnp.exp2(nt(protos_ref[here, :], rows) * (LOG2E / student_temp))
        grads_ref[...] += nn(protos_t_ref[:, here], values.astype(bf16))
        return total + jnp.sum(values.reshape(BLOCK // 8, 8, T), axis=0)

    total = lax.fori_loop(0, K // BLOCK, step, jnp.zeros((8, T), f32), unroll=4)
    store_packed(total_ref, 0, jnp.sum(total, axis=0, keepdims=True))


def student_proto_kernel(protos_ref, rows_ref, rows_t_ref, total_ref, weight_ref, out_ref):
    rows = rows_ref[...]
    scale = as_row(weight_ref[...] / (student_temp * total_ref[...]))
    right = (rows_t_ref[...].astype(f32) * scale).astype(bf16)

    def step(b, carry):
        here = pl.ds(pl.multiple_of(b * BLOCK, BLOCK), BLOCK)
        values = jnp.exp2(nt(protos_ref[here, :], rows) * (LOG2E / student_temp))
        out_ref[here, :] = nt(values.astype(bf16), right).astype(bf16)
        return carry

    lax.fori_loop(0, K // BLOCK, step, 0, unroll=4)


def store_copies(ref, start, row):
    for j in range(row.shape[1] // LANES):
        piece = row[:, j * LANES : (j + 1) * LANES]
        for copy in range(GROUPS):
            ref[copy, start + j : start + j + 1, :] = piece


def token_mass(packed, exp_ref, mass_ref):
    scale = three_rows(as_row(packed))
    total = jnp.zeros((16, T), f32)
    for b in range(K // BLOCK):
        here = slice(b * BLOCK, (b + 1) * BLOCK)
        total = total + nn(scale[:, here], exp_ref[here, :])
    store_copies(mass_ref, 0, jnp.sum(total, axis=0, keepdims=True))


def first_token_mass_kernel(near_ref, far_ref, exp_ref, mass_ref):
    token_mass(1.0 / (near_ref[...] + far_ref[...]), exp_ref, mass_ref)


def token_mass_kernel(near_ref, far_ref, exp_ref, student_ref, mass_ref):
    token_mass(1.0 / (near_ref[...] + far_ref[...]), exp_ref, mass_ref)
    student = student_ref[...]
    for copy in range(GROUPS):
        mass_ref[copy, PACKED : 2 * PACKED, :] = student


def last_token_mass_kernel(
    near_ref, far_ref, exp_ref, protos_t_ref, rows_t_ref, mass_ref, scale_ref, grads_ref, left_ref
):
    packed = 1.0 / (near_ref[...] + far_ref[...])
    scale_ref[...] = packed
    scale = as_row(packed)
    left_ref[D : D + 16, :] = three_rows(scale)
    left_ref[0:D, :] = (protos_t_ref[...].astype(f32) * scale).astype(bf16)
    for j in range(T // BLOCK):
        here = slice(j * BLOCK, (j + 1) * BLOCK)
        both = nn(left_ref[...], exp_ref[:, here])
        grads = both[0:D]
        grads_ref[:, here] = grads
        store_copies(mass_ref, j * BLOCK // LANES, jnp.sum(both[D:], axis=0, keepdims=True))
        cross = jnp.sum(grads * rows_t_ref[:, here].astype(f32), axis=0, keepdims=True)
        store_copies(mass_ref, (T + j * BLOCK) // LANES, cross)


def column_mass(scale, exp_ref, mass_ref):
    split = three_rows(scale)
    for b in range(K // 1024):
        start = b * 1024 + 640
        row = jnp.sum(nt(split, exp_ref[start : start + 384, :]), axis=0, keepdims=True)
        store_packed(mass_ref, start // LANES, row)
        start = b * 1024
        part = jnp.zeros((640, LANES), f32)
        for j in range(T // LANES):
            lanes = slice(j * LANES, (j + 1) * LANES)
            part = part + exp_ref[start : start + 640, lanes].astype(f32) * scale[:, lanes]
        store_packed(mass_ref, start // LANES, jnp.sum(jnp.transpose(part), axis=0, keepdims=True))


def first_proto_mass_kernel(parts_ref, exp_ref, mass_ref):
    column_mass(1.0 / as_row(jnp.sum(parts_ref[...], axis=0)), exp_ref, mass_ref)


def proto_mass_kernel(parts_ref, exp_ref, mass_ref, total_ref):
    parts = jnp.sum(parts_ref[...], axis=0)
    total_ref[...] = parts[PACKED:]
    column_mass(1.0 / as_row(parts[0:PACKED]), exp_ref, mass_ref)


def combine_kernel(
    place_ref, parts_ref, total_ref, weight_ref, student_ref, teacher_ref,
    loss_ref, scale_ref, keep_ref, one_ref, two_ref, three_ref, rows_ref
):
    parts = jnp.sum(parts_ref[...], axis=0)
    token_scale = 1.0 / parts[0:PACKED]
    total, weight = total_ref[...], weight_ref[...]
    cross = jnp.log(total) - token_scale * parts[PACKED:] / student_temp
    loss_ref[...] = jnp.full((8, LANES), jnp.sum(weight * cross) / TOKENS, f32)
    teacher_scale = weight * token_scale / student_temp
    scale_ref[...] = teacher_scale
    rows_ref[0:1, :] = as_row(weight / (student_temp * total))
    rows_ref[8:9, :] = as_row(teacher_scale)
    for step, ref in enumerate((keep_ref, one_ref, two_ref, three_ref)):
        block = lax.rem(place_ref[2] + step, 4)
        here = pl.ds(pl.multiple_of(block * 256, 256), 256)
        grads = student_ref[:, here] * rows_ref[0:1, here] - teacher_ref[:, here] * rows_ref[8:9, here]
        ref[...] = jnp.transpose(grads).astype(ref.dtype)


def fold_rows_kernel(place_ref, own_ref, a_ref, b_ref, c_ref, keep_ref, one_ref, two_ref, three_ref):
    for step, ref in enumerate((keep_ref, one_ref, two_ref, three_ref)):
        block = lax.rem(place_ref[3] + step, 4)
        here = pl.ds(pl.multiple_of(block * 64, 64), 64)
        total = own_ref[here, :] + a_ref[here, :].astype(f32) + b_ref[here, :].astype(f32)
        ref[...] = (total + c_ref[here, :].astype(f32)).astype(ref.dtype)


def proto_kernel(chunks, place_ref, loss_ref, teacher_scale_ref, scale_ref, rows_t_ref, exp_ref, student_ref, *outs):
    right = (rows_t_ref[...].astype(f32) * as_row(teacher_scale_ref[...])).astype(bf16)
    places = [(ref, i * 1024) for ref in outs for i in range(ref.shape[0] // 1024)]
    for (z_step, core_flip), (ref, first) in zip(chunks, places):
        z = lax.rem(place_ref[0] + z_step, 4)
        core = 1 - place_ref[1] if core_flip else place_ref[1]
        chunk = z * 2 + core
        if ref.shape[0] == 1040:
            ref[1024:1040, :] = loss_rows(loss_ref[0:1, :])
        for b in range(2):
            start = pl.multiple_of(chunk * 1024 + b * 512, 512)
            product = nt(exp_ref[pl.ds(start, 512), :], right)
            student = student_ref[pl.ds(start, 512), :].astype(f32)
            for j in range(4):
                row = scale_ref[pl.ds(chunk * 8 + b * 4 + j, 1), :]
                column = jnp.transpose(jnp.broadcast_to(row, (LANES, LANES)))
                column = jnp.concatenate([column, column], axis=1)
                here = slice(j * LANES, (j + 1) * LANES)
                value = student[here] - product[here] * column
                to = first + b * 512 + j * LANES
                ref[to : to + LANES, :] = value.astype(ref.dtype)


def loss_rows(row):
    return three_rows(jnp.concatenate([row, row], axis=1))


def loss_of(rows):
    return jnp.sum(rows.astype(f32), axis=0, keepdims=True)[:, 0:LANES]


def first_fold_kernel(own_ref, core_ref, loss_ref, up_ref, down_ref, loss_out_ref):
    loss = loss_ref[0:1, :] + loss_of(core_ref[1024:1040, :])
    loss_out_ref[...] = jnp.broadcast_to(loss, (8, LANES))
    for i, ref in enumerate((up_ref, down_ref)):
        here = slice(i * 512, (i + 1) * 512)
        ref[0:512, :] = (own_ref[here, :] + core_ref[here, :].astype(f32)).astype(bf16)
        ref[512:528, :] = loss_rows(loss)


def second_fold_kernel(own_ref, core_ref, up_ref, down_ref, next_ref, last_ref):
    for i in range(4):
        here = slice(i * 512, (i + 1) * 512)
        value = own_ref[here, :] + core_ref[here, :].astype(f32)
        if i in (0, 3):
            value = value + (up_ref if i == 0 else down_ref)[0:512, :].astype(f32)
        to = i % 2 * 512
        (next_ref if i < 2 else last_ref)[to : to + 512, :] = value.astype(bf16)
    next_ref[1024:1040, :] = up_ref[512:528, :]
    last_ref[1024:1040, :] = up_ref[512:528, :]


def normalize_back(unit, scale, grad):
    return scale * (grad - unit * jnp.sum(unit * grad, axis=-1, keepdims=True))


def own_kernel(place_ref, far_weight_ref, own_ref, core_ref, unit_ref, scale_ref, base_ref, weight_ref, arrived):
    start = pl.multiple_of((place_ref[0] * 2 + place_ref[1]) * 1024, 1024)
    read = pltpu.make_async_copy(far_weight_ref.at[pl.ds(start, 1024), :], weight_ref, arrived)
    read.start()
    base_ref[...] = own_ref[2048:3072, :] + core_ref[2048:3072, :].astype(f32)
    read.wait()
    unit, scale = normalize_rows(weight_ref[...].astype(f32))
    unit_ref[...] = unit
    scale_ref[...] = jnp.broadcast_to(scale, (1024, LANES))


def weight_grads_kernel(
    unit_ref, scale_ref, base_ref, loss_ref, up_ref, down_ref, last_ref, next_ref, out_ref, loss_out_ref
):
    far = loss_ref[0:1, :] + loss_of(last_ref[1024:1040, :])
    loss = far + (loss_of(up_ref[512:528, :]) + loss_of(down_ref[512:528, :]))
    loss_out_ref[...] = loss[:, 0:1]
    grads = base_ref[...] + (last_ref[0:1024, :].astype(f32) + next_ref[0:1024, :].astype(f32))
    out_ref[...] = normalize_back(unit_ref[...], scale_ref[:, 0:1], grads)


def feature_grads_kernel(rows_ref, own_ref, a_ref, b_ref, c_ref, out_ref):
    grads = own_ref[...] + a_ref[...].astype(f32) + b_ref[...].astype(f32) + c_ref[...].astype(f32)
    unit, scale = normalize_rows(rows_ref[...])
    out_ref[...] = normalize_back(unit, scale, grads)


def turn(values, axis, step):
    return lax.ppermute(values, axis, [(i, (i + step) % 4) for i in range(4)])


def flip(values, axis):
    return lax.ppermute(values, axis, [(0, 1), (1, 0)])


def over_token_groups(values):
    pairs = [(i, i ^ 1) for i in range(4)]
    both = [(z * 2 + c, (z ^ 1) * 2 + (1 - c)) for z in range(4) for c in range(2)]
    near = (values + flip(values, "c")) + (lax.ppermute(values, "z", pairs) + lax.ppermute(values, ("z", "c"), both))
    return near, lax.ppermute(near, "z", [(i, 3 - i) for i in range(4)])


def exchange(blocks):
    return lax.all_to_all(blocks, SAME_TOKENS, 0, 0, tiled=True)


def local(student_patches, teacher_patches, mask_positions, token_weight, student_weight, teacher_weight):
    z, c, y, x = (lax.axis_index(name) for name in ("z", "c", "y", "x"))
    place = jnp.stack([z, c, y, x]).astype(jnp.int32)
    matrix = K * T * 2
    product = 2 * K * T * D
    shape = jax.ShapeDtypeStruct
    row, rows = shape((PACKED, LANES), f32), shape((K // LANES, LANES), f32)
    resident = pltpu.VMEM((K, T), bf16)

    DMA = pltpu.SemaphoreType.DMA
    unit_rows, student_rows = call(
        rows_kernel, [shape((144, D), bf16), shape((64, D), f32)],
        teacher_patches, student_patches, mask_positions, token_weight, far=(0, 1, 2, 3),
        scratch=[
            pltpu.VMEM((2, 256, D), bf16), pltpu.VMEM((2, 256, D), bf16),
            pltpu.VMEM((2, 32), jnp.int32), pltpu.VMEM((2, 32), bf16), DMA((4,)),
        ],
        name="rows",
    )
    unit_rows, place = lax.optimization_barrier((unit_rows, place))
    parts = [unit_rows] + [turn(unit_rows, "y", i) for i in (1, 2, 3)]
    protos = pltpu.VMEM((K, D), bf16)
    loading = dict(far=(0,), scratch=[protos, DMA((K // BLOCK,))])
    (teacher_protos,) = call(protos_kernel, [protos], teacher_weight, name="teacher_protos", moved=2 * K * D, **loading)
    *parts, teacher_protos = lax.optimization_barrier((*parts, teacher_protos))
    column = jnp.concatenate(parts, axis=0)
    halves = jnp.concatenate(parts[0:2], axis=0), jnp.concatenate(parts[2:4], axis=0)
    gathered = [column, turn(column, "x", 1), *(turn(half, "x", 2) for half in halves), turn(column, "x", 3)]
    student_protos, protos_t = call(
        protos_t_kernel, [shape((K, D), bf16), shape((D, K), bf16)], student_weight,
        name="student_protos", moved=2 * K * D, **loading,
    )
    *gathered, student_protos = lax.optimization_barrier((*gathered, student_protos))
    teacher_exp, mass = call(
        teacher_kernel, [resident, rows], place, *gathered, teacher_protos,
        scratch=[pltpu.VMEM((T, D), bf16)], limit=16, name="teacher_exp",
    )
    masses = over_token_groups(mass)
    total, student_all, rows_t, weight, student_part = call(
        student_kernel,
        [row, shape((T, D), bf16), shape((D, T), bf16), row, shape((D, T), f32)],
        place, *gathered, student_protos, protos_t,
        scratch=[pltpu.VMEM((GROUPS, 16, LANES), f32)],
        limit=16, name="student_unit_grads", flops=2 * product, moved=matrix, exps=K * T,
    )
    (copies,) = call(
        first_token_mass_kernel, [shape((GROUPS, PACKED, LANES), f32)], *masses, teacher_exp,
        name="token_mass", moved=matrix // 2,
    )
    copies, total, student_part = lax.optimization_barrier((copies, total, student_part))
    parts = exchange(copies)
    (mass,) = call(
        first_proto_mass_kernel, [rows], parts, teacher_exp, name="proto_mass", moved=matrix // 2
    )
    masses = over_token_groups(mass)
    (copies,) = call(
        token_mass_kernel, [shape((GROUPS, 2 * PACKED, LANES), f32)], *masses, teacher_exp, total,
        name="token_mass", moved=matrix // 2,
    )
    parts = exchange(copies)
    mass, total = call(
        proto_mass_kernel, [rows, row], parts, teacher_exp, name="proto_mass", moved=matrix // 2
    )
    masses = over_token_groups(mass)
    (student_proto,) = call(
        student_proto_kernel, [shape((K, D), bf16)], student_protos, student_all, rows_t, total, weight,
        limit=16, name="student_proto_grads", flops=2 * product, moved=matrix, exps=K * T,
    )
    copies, proto_scale, teacher_part = call(
        last_token_mass_kernel,
        [shape((GROUPS, 2 * PACKED, LANES), f32), rows, shape((D, T), f32)],
        *masses, teacher_exp, protos_t, rows_t,
        scratch=[pltpu.VMEM((D + 16, K), bf16)], limit=12, name="last_token_mass", flops=product, moved=matrix,
    )
    copies, student_proto = lax.optimization_barrier((copies, student_proto))
    parts = exchange(copies)
    loss, teacher_scale, own, one, two, three = call(
        combine_kernel,
        [shape((8, LANES), f32), row, shape((256, D), f32)] + [shape((256, D), bf16)] * 3,
        place, parts, total, weight, student_part, teacher_part,
        scratch=[pltpu.VMEM((16, T), f32)], name="combine",
    )
    one, two, three = turn(one, "y", 1), turn(two, "y", 2), turn(three, "y", 3)

    def proto_grads(name, chunks, outs):
        return call(
            lambda *refs: proto_kernel(chunks, *refs), outs,
            place, loss, teacher_scale, proto_scale, rows_t, teacher_exp, student_proto,
            name=name,
        )

    keep = shape((1024, D), f32)
    (far,) = proto_grads("proto_grads_far_send", [(2, True)], [shape((1040, D), bf16)])
    from_far = flip(far, "c")
    teacher_scale, far = lax.optimization_barrier((teacher_scale, far))
    (far_keep,) = proto_grads("proto_grads_far_keep", [(2, False)], [keep])
    piece, side = shape((528, D), bf16), shape((1040, D), bf16)
    up, down, loss_here = call(
        first_fold_kernel, [piece, piece, shape((8, LANES), f32)], far_keep, from_far, loss, name="first_fold",
    )
    up_there, down_there = turn(up, "z", 1), turn(down, "z", 3)
    teacher_scale, loss_here = lax.optimization_barrier((teacher_scale, loss_here))
    (others,) = proto_grads("proto_grads_send", [(1, True), (3, True), (0, True)], [shape((3072, D), bf16)])
    others, teacher_scale, up_there, down_there, one, two, three = lax.optimization_barrier(
        (others, teacher_scale, up_there, down_there, one, two, three)
    )
    from_others = flip(others, "c")
    (others_keep,) = proto_grads("proto_grads_keep", [(1, False), (3, False), (0, False)], [shape((3072, D), f32)])
    own, others_keep = lax.optimization_barrier((own, others_keep))
    own, one, two, three = call(
        fold_rows_kernel, [shape((64, D), f32)] + [shape((64, D), bf16)] * 3,
        place, own, one, two, three, name="fold_rows",
    )
    first, second = call(
        second_fold_kernel, [side, side], others_keep, from_others, up_there, down_there, name="second_fold",
    )
    own, first = lax.optimization_barrier((own, first))
    one, two, three = turn(one, "x", 1), turn(two, "x", 2), turn(three, "x", 3)
    from_last, from_next = turn(first, "z", 1), turn(second, "z", 3)
    unit, scale, base = call(
        own_kernel, [keep, shape((1024, LANES), f32), keep], place, student_weight, others_keep, from_others, far=(1,),
        scratch=[pltpu.VMEM((1024, D), bf16), DMA], name="own",
    )
    (feature_grads,) = call(
        feature_grads_kernel, [shape((64, D), f32)], student_rows, own, one, two, three, name="feature_grads",
    )
    weight_grads, loss = call(
        weight_grads_kernel, [keep, shape((1, 1), f32)],
        unit, scale, base, loss_here, up_there, down_there, from_last, from_next, name="weight_grads",
    )
    return loss.reshape(()), feature_grads.reshape(2, 32, D), weight_grads


def solution(mesh):
    fine = Mesh(mesh.devices.reshape(4, 2, 4, 4), ("z", "c", "y", "x"))
    every, proto = ("z", "c", "y", "x"), ("y", "x")
    return jax.shard_map(
        local,
        mesh=fine,
        in_specs=(
            P(every, None, None),
            P(every, None, None),
            P(every, None),
            P(every, None),
            P(proto, None),
            P(proto, None),
        ),
        out_specs=(P(), P(every, None, None), P(("y", "x", "z", "c"), None)),
        check_vma=False,
    )
```

```python
import jax
import jax.numpy as jnp
from jax import lax
from jax.experimental import pallas as pl
from jax.experimental.pallas import tpu as pltpu
from jax.sharding import Mesh, PartitionSpec as P

teacher_temp = 0.07
student_temp = 0.1
epsilon = 1e-06
LOG2E = 1.4426950408889634
SWEEPS = 3
TOKENS = 8192
T, K, D = 1024, 8192, 256
BLOCK = 512
HALF = 8
LANES = 128
f32, bf16 = jnp.float32, jnp.bfloat16
GROUPS = 16
PACKED = T // LANES
SAME_TOKENS = ("y", "x")
VMEM = pl.BlockSpec(memory_space=pltpu.VMEM)
SMEM = pl.BlockSpec(memory_space=pltpu.SMEM)


def nt(left, right):
    return lax.dot_general(left, right, (((1,), (1,)), ((), ())), preferred_element_type=f32)


def nn(left, right):
    return lax.dot_general(left, right, (((1,), (0,)), ((), ())), preferred_element_type=f32)


def normalize_rows(values):
    scale = lax.rsqrt(jnp.sum(values * values, axis=-1, keepdims=True) + epsilon)
    return values * scale, scale


def three_rows(row):
    high = row.astype(bf16).astype(f32)
    rest = row - high
    middle = rest.astype(bf16).astype(f32)
    low = rest - middle
    index = lax.broadcasted_iota(jnp.int32, (16, row.shape[1]), 0)
    picked = jnp.where(index == 0, high, jnp.where(index == 1, middle, jnp.where(index == 2, low, 0.0)))
    return picked.astype(bf16)


def as_row(packed):
    return jnp.concatenate([packed[j : j + 1, :] for j in range(packed.shape[0])], axis=1)


def store_packed(ref, start, row):
    for j in range(row.shape[1] // LANES):
        ref[start + j : start + j + 1, :] = row[:, j * LANES : (j + 1) * LANES]


def call(kernel, outs, *args, far=(), aliases=None, scratch=(), limit=11, name=None, flops=0, moved=0, exps=0):
    specs = [SMEM if arg.dtype == jnp.int32 and arg.ndim == 1 else VMEM for arg in args]
    args = list(args)
    for i in far:
        specs[i] = pl.BlockSpec(memory_space=pl.ANY)
        args[i] = pltpu.with_memory_space_constraint(args[i], pltpu.HBM)
    return pl.pallas_call(
        kernel,
        out_shape=outs,
        in_specs=specs,
        out_specs=[VMEM] * len(outs),
        scratch_shapes=list(scratch),
        input_output_aliases=aliases or {},
        compiler_params=pltpu.CompilerParams(vmem_limit_bytes=limit << 20),
        cost_estimate=pl.CostEstimate(flops=flops, bytes_accessed=moved, transcendentals=exps),
        name=name,
    )(*args)


def lane_sums(values):
    part = values[:, 0:LANES]
    for j in range(1, values.shape[1] // LANES):
        part = part + values[:, j * LANES : (j + 1) * LANES]
    return jnp.sum(jnp.transpose(part), axis=0, keepdims=True)


def pick_rows(patches_ref, positions_ref, image):
    patch = lax.broadcasted_iota(jnp.int32, (256, 32), 0)
    chosen = (patch == positions_ref[image : image + 1, :]).astype(f32).astype(bf16)
    return lax.dot_general(chosen, patches_ref[image], (((0,), (0,)), ((), ())), preferred_element_type=f32)


def rows_kernel(
    far_teacher_ref, far_student_ref, far_positions_ref, far_weight_ref, unit_ref, rows_ref,
    teacher_ref, student_ref, positions_ref, weight_ref, arrived
):
    pairs = (
        (far_positions_ref, positions_ref), (far_teacher_ref, teacher_ref),
        (far_student_ref, student_ref), (far_weight_ref, weight_ref),
    )
    reads = [pltpu.make_async_copy(far, near, arrived.at[i]) for i, (far, near) in enumerate(pairs)]
    for read in reads:
        read.start()
    reads[0].wait()
    reads[1].wait()
    for image in range(2):
        here = slice(image * 32, (image + 1) * 32)
        unit_ref[here, :] = normalize_rows(pick_rows(teacher_ref, positions_ref, image))[0].astype(bf16)
    reads[2].wait()
    for image in range(2):
        here = slice(image * 32, (image + 1) * 32)
        rows = pick_rows(student_ref, positions_ref, image)
        rows_ref[here, :] = rows
        unit_ref[64 + image * 32 : 96 + image * 32, :] = normalize_rows(rows)[0].astype(bf16)
    reads[3].wait()
    row = lax.broadcasted_iota(jnp.int32, (16, 32), 0)
    weight = weight_ref[...].astype(f32)
    weight = jnp.where(row == 0, weight[0:1], jnp.where(row == 1, weight[1:2], 0.0)).astype(bf16)
    same = lax.broadcasted_iota(jnp.int32, (32, D), 0) == lax.broadcasted_iota(jnp.int32, (32, D), 1)
    unit_ref[128:144, :] = nn(weight, same.astype(f32).astype(bf16)).astype(bf16)


def source(place_ref, y_step, x_step):
    return lax.rem(place_ref[2] + 4 - y_step, 4) * 4 + lax.rem(place_ref[3] + 4 - x_step, 4)


def fetch(far_ref, near_ref, arrived):
    reads = [
        pltpu.make_async_copy(
            far_ref.at[pl.ds(b * BLOCK, BLOCK), :], near_ref.at[pl.ds(b * BLOCK, BLOCK), :], arrived.at[b]
        )
        for b in range(K // BLOCK)
    ]
    for read in reads:
        read.start()
    return reads


def protos_kernel(far_weight_ref, out_ref, weight_ref, arrived):
    for b, read in enumerate(fetch(far_weight_ref, weight_ref, arrived)):
        here = slice(b * BLOCK, (b + 1) * BLOCK)
        read.wait()
        out_ref[here, :] = normalize_rows(weight_ref[here, :].astype(f32))[0].astype(bf16)


def protos_t_kernel(far_weight_ref, out_ref, out_t_ref, weight_ref, arrived):
    for b, read in enumerate(fetch(far_weight_ref, weight_ref, arrived)):
        here = slice(b * BLOCK, (b + 1) * BLOCK)
        read.wait()
        protos = normalize_rows(weight_ref[here, :].astype(f32))[0].astype(bf16)
        out_ref[here, :] = protos
        out_t_ref[:, here] = jnp.transpose(protos.astype(f32)).astype(bf16)


def gathered_blocks(place_ref, a_ref, b_ref, c_ref, c2_ref, d_ref):
    for x_step, refs in enumerate(((a_ref,), (b_ref,), (c_ref, c2_ref), (d_ref,))):
        for y_step in range(4):
            ref, at = refs[y_step * len(refs) // 4], y_step % (4 // len(refs)) * 144
            yield source(place_ref, y_step, x_step), ref, at


def teacher_kernel(place_ref, a_ref, b_ref, c_ref, c2_ref, d_ref, protos_ref, exp_ref, mass_ref, rows_ref):
    for place, ref, at in gathered_blocks(place_ref, a_ref, b_ref, c_ref, c2_ref, d_ref):
        rows_ref[pl.ds(pl.multiple_of(place * 64, 64), 64), :] = ref[at : at + 64, :]
    rows = rows_ref[...]
    for b in range(K // BLOCK):
        here = slice(b * BLOCK, (b + 1) * BLOCK)
        values = jnp.exp2(nt(protos_ref[here, :], rows) * (LOG2E / teacher_temp))
        exp_ref[here, :] = values.astype(bf16)
        store_packed(mass_ref, b * BLOCK // LANES, lane_sums(values))


def student_kernel(
    place_ref, a_ref, b_ref, c_ref, c2_ref, d_ref, protos_ref, protos_t_ref,
    total_ref, rows_ref, rows_t_ref, token_weight_ref, grads_ref, extra_ref
):
    for place, ref, at in gathered_blocks(place_ref, a_ref, b_ref, c_ref, c2_ref, d_ref):
        rows_ref[pl.ds(pl.multiple_of(place * 64, 64), 64), :] = ref[at + 64 : at + 128, :]
        extra_ref[pl.ds(place, 1)] = ref[at + 128 : at + 144, 0:LANES].astype(f32)[None]
    rows = rows_ref[...]
    rows_t_ref[...] = jnp.transpose(rows.astype(f32)).astype(bf16)
    for j in range(PACKED):
        row = jnp.zeros((1, LANES), f32)
        for piece in range(4):
            row = row + pltpu.roll(extra_ref[2 * j + piece // 2], piece * 32, 1)[piece % 2 : piece % 2 + 1]
        token_weight_ref[j : j + 1, :] = row
    grads_ref[...] = jnp.zeros_like(grads_ref)
    total = jnp.zeros((8, T), f32)
    total_ref[...] = student_blocks(0, HALF, rows, protos_ref, protos_t_ref, grads_ref, total)


def student_blocks(first, last, rows, protos_ref, protos_t_ref, grads_ref, total):
    def step(b, total):
        here = pl.ds(pl.multiple_of(b * BLOCK, BLOCK), BLOCK)
        values = jnp.exp2(nt(protos_ref[here, :], rows) * (LOG2E / student_temp))
        grads_ref[...] += nn(protos_t_ref[:, here], values.astype(bf16))
        return total + jnp.sum(values.reshape(BLOCK // 8, 8, T), axis=0)

    return lax.fori_loop(first, last, step, total, unroll=4)


def student_rest_kernel(rows_ref, protos_ref, protos_t_ref, part_ref, early_ref, total_ref, grads_ref):
    grads_ref[...] = early_ref[...]
    total = student_blocks(HALF, K // BLOCK, rows_ref[...], protos_ref, protos_t_ref, grads_ref, part_ref[...])
    store_packed(total_ref, 0, jnp.sum(total, axis=0, keepdims=True))


def student_proto_rest_kernel(protos_ref, rows_ref, rows_t_ref, total_ref, weight_ref, held_ref, out_ref):
    student_proto_blocks(HALF, K // BLOCK, protos_ref, rows_ref, rows_t_ref, total_ref, weight_ref, out_ref)


def student_proto_kernel(*refs):
    student_proto_blocks(0, HALF, *refs)


def student_proto_blocks(first, last, protos_ref, rows_ref, rows_t_ref, total_ref, weight_ref, out_ref):
    rows = rows_ref[...]
    scale = as_row(weight_ref[...] / (student_temp * total_ref[...]))
    right = (rows_t_ref[...].astype(f32) * scale).astype(bf16)

    def step(b, carry):
        here = pl.ds(pl.multiple_of(b * BLOCK, BLOCK), BLOCK)
        values = jnp.exp2(nt(protos_ref[here, :], rows) * (LOG2E / student_temp))
        out_ref[here, :] = nt(values.astype(bf16), right).astype(bf16)
        return carry

    lax.fori_loop(first, last, step, 0, unroll=4)


def store_copies(ref, start, row):
    for j in range(row.shape[1] // LANES):
        piece = row[:, j * LANES : (j + 1) * LANES]
        for copy in range(GROUPS):
            ref[copy, start + j : start + j + 1, :] = piece


def token_mass(packed, exp_ref, mass_ref):
    scale = three_rows(as_row(packed))
    total = jnp.zeros((16, T), f32)
    for b in range(K // BLOCK):
        here = slice(b * BLOCK, (b + 1) * BLOCK)
        total = total + nn(scale[:, here], exp_ref[here, :])
    store_copies(mass_ref, 0, jnp.sum(total, axis=0, keepdims=True))


def first_token_mass_kernel(near_ref, far_ref, exp_ref, mass_ref):
    token_mass(1.0 / (near_ref[...] + far_ref[...]), exp_ref, mass_ref)


def token_mass_kernel(near_ref, far_ref, exp_ref, student_ref, mass_ref):
    token_mass(1.0 / (near_ref[...] + far_ref[...]), exp_ref, mass_ref)
    student = student_ref[...]
    for copy in range(GROUPS):
        mass_ref[copy, PACKED : 2 * PACKED, :] = student


def last_token_mass_kernel(
    near_ref, far_ref, exp_ref, protos_t_ref, rows_t_ref, mass_ref, scale_ref, grads_ref, left_ref
):
    packed = 1.0 / (near_ref[...] + far_ref[...])
    scale_ref[...] = packed
    scale = as_row(packed)
    left_ref[D : D + 16, :] = three_rows(scale)
    left_ref[0:D, :] = (protos_t_ref[...].astype(f32) * scale).astype(bf16)
    for j in range(T // BLOCK):
        here = slice(j * BLOCK, (j + 1) * BLOCK)
        both = nn(left_ref[...], exp_ref[:, here])
        grads = both[0:D]
        grads_ref[:, here] = grads
        store_copies(mass_ref, j * BLOCK // LANES, jnp.sum(both[D:], axis=0, keepdims=True))
        cross = jnp.sum(grads * rows_t_ref[:, here].astype(f32), axis=0, keepdims=True)
        store_copies(mass_ref, (T + j * BLOCK) // LANES, cross)


def column_mass(scale, exp_ref, mass_ref):
    split = three_rows(scale)
    for b in range(K // 1024):
        start = b * 1024 + 640
        row = jnp.sum(nt(split, exp_ref[start : start + 384, :]), axis=0, keepdims=True)
        store_packed(mass_ref, start // LANES, row)
        start = b * 1024
        part = jnp.zeros((640, LANES), f32)
        for j in range(T // LANES):
            lanes = slice(j * LANES, (j + 1) * LANES)
            part = part + exp_ref[start : start + 640, lanes].astype(f32) * scale[:, lanes]
        store_packed(mass_ref, start // LANES, jnp.sum(jnp.transpose(part), axis=0, keepdims=True))


def first_proto_mass_kernel(parts_ref, exp_ref, mass_ref):
    column_mass(1.0 / as_row(jnp.sum(parts_ref[...], axis=0)), exp_ref, mass_ref)


def proto_mass_kernel(parts_ref, exp_ref, mass_ref, total_ref):
    parts = jnp.sum(parts_ref[...], axis=0)
    total_ref[...] = parts[PACKED:]
    column_mass(1.0 / as_row(parts[0:PACKED]), exp_ref, mass_ref)


def combine_kernel(
    place_ref, parts_ref, total_ref, weight_ref, student_ref, teacher_ref,
    loss_ref, scale_ref, keep_ref, one_ref, two_ref, three_ref, rows_ref
):
    parts = jnp.sum(parts_ref[...], axis=0)
    token_scale = 1.0 / parts[0:PACKED]
    total, weight = total_ref[...], weight_ref[...]
    cross = jnp.log(total) - token_scale * parts[PACKED:] / student_temp
    loss_ref[...] = jnp.full((8, LANES), jnp.sum(weight * cross) / TOKENS, f32)
    teacher_scale = weight * token_scale / student_temp
    scale_ref[...] = teacher_scale
    rows_ref[0:1, :] = as_row(weight / (student_temp * total))
    rows_ref[8:9, :] = as_row(teacher_scale)
    for step, ref in enumerate((keep_ref, one_ref, two_ref, three_ref)):
        block = lax.rem(place_ref[2] + step, 4)
        here = pl.ds(pl.multiple_of(block * 256, 256), 256)
        grads = student_ref[:, here] * rows_ref[0:1, here] - teacher_ref[:, here] * rows_ref[8:9, here]
        ref[...] = jnp.transpose(grads).astype(ref.dtype)


def fold_rows_kernel(place_ref, own_ref, a_ref, b_ref, c_ref, keep_ref, one_ref, two_ref, three_ref):
    for step, ref in enumerate((keep_ref, one_ref, two_ref, three_ref)):
        block = lax.rem(place_ref[3] + step, 4)
        here = pl.ds(pl.multiple_of(block * 64, 64), 64)
        total = own_ref[here, :] + a_ref[here, :].astype(f32) + b_ref[here, :].astype(f32)
        ref[...] = (total + c_ref[here, :].astype(f32)).astype(ref.dtype)


def proto_kernel(chunks, place_ref, loss_ref, teacher_scale_ref, scale_ref, rows_t_ref, exp_ref, student_ref, *outs):
    right = (rows_t_ref[...].astype(f32) * as_row(teacher_scale_ref[...])).astype(bf16)
    places = [(ref, i * 1024) for ref in outs for i in range(ref.shape[0] // 1024)]
    for (z_step, core_flip), (ref, first) in zip(chunks, places):
        z = lax.rem(place_ref[0] + z_step, 4)
        core = 1 - place_ref[1] if core_flip else place_ref[1]
        chunk = z * 2 + core
        if ref.shape[0] == 1040:
            ref[1024:1040, :] = loss_rows(loss_ref[0:1, :])
        for b in range(2):
            start = pl.multiple_of(chunk * 1024 + b * 512, 512)
            product = nt(exp_ref[pl.ds(start, 512), :], right)
            student = student_ref[pl.ds(start, 512), :].astype(f32)
            for j in range(4):
                row = scale_ref[pl.ds(chunk * 8 + b * 4 + j, 1), :]
                column = jnp.transpose(jnp.broadcast_to(row, (LANES, LANES)))
                column = jnp.concatenate([column, column], axis=1)
                here = slice(j * LANES, (j + 1) * LANES)
                value = student[here] - product[here] * column
                to = first + b * 512 + j * LANES
                ref[to : to + LANES, :] = value.astype(ref.dtype)


def loss_rows(row):
    return three_rows(jnp.concatenate([row, row], axis=1))


def loss_of(rows):
    return jnp.sum(rows.astype(f32), axis=0, keepdims=True)[:, 0:LANES]


def first_fold_kernel(own_ref, core_ref, loss_ref, up_ref, down_ref, loss_out_ref):
    loss = loss_ref[0:1, :] + loss_of(core_ref[1024:1040, :])
    loss_out_ref[...] = jnp.broadcast_to(loss, (8, LANES))
    for i, ref in enumerate((up_ref, down_ref)):
        here = slice(i * 512, (i + 1) * 512)
        ref[0:512, :] = (own_ref[here, :] + core_ref[here, :].astype(f32)).astype(bf16)
        ref[512:528, :] = loss_rows(loss)


def second_fold_kernel(own_ref, core_ref, up_ref, down_ref, next_ref, last_ref):
    for i in range(4):
        here = slice(i * 512, (i + 1) * 512)
        value = own_ref[here, :] + core_ref[here, :].astype(f32)
        if i in (0, 3):
            value = value + (up_ref if i == 0 else down_ref)[0:512, :].astype(f32)
        to = i % 2 * 512
        (next_ref if i < 2 else last_ref)[to : to + 512, :] = value.astype(bf16)
    next_ref[1024:1040, :] = up_ref[512:528, :]
    last_ref[1024:1040, :] = up_ref[512:528, :]


def normalize_back(unit, scale, grad):
    return scale * (grad - unit * jnp.sum(unit * grad, axis=-1, keepdims=True))


def own_kernel(place_ref, far_weight_ref, own_ref, core_ref, unit_ref, scale_ref, base_ref, weight_ref, arrived):
    start = pl.multiple_of((place_ref[0] * 2 + place_ref[1]) * 1024, 1024)
    read = pltpu.make_async_copy(far_weight_ref.at[pl.ds(start, 1024), :], weight_ref, arrived)
    read.start()
    base_ref[...] = own_ref[2048:3072, :] + core_ref[2048:3072, :].astype(f32)
    read.wait()
    unit, scale = normalize_rows(weight_ref[...].astype(f32))
    unit_ref[...] = unit
    scale_ref[...] = jnp.broadcast_to(scale, (1024, LANES))


def weight_grads_kernel(
    unit_ref, scale_ref, base_ref, loss_ref, up_ref, down_ref, last_ref, next_ref, out_ref, loss_out_ref
):
    far = loss_ref[0:1, :] + loss_of(last_ref[1024:1040, :])
    loss = far + (loss_of(up_ref[512:528, :]) + loss_of(down_ref[512:528, :]))
    loss_out_ref[...] = loss[:, 0:1]
    grads = base_ref[...] + (last_ref[0:1024, :].astype(f32) + next_ref[0:1024, :].astype(f32))
    out_ref[...] = normalize_back(unit_ref[...], scale_ref[:, 0:1], grads)


def feature_grads_kernel(rows_ref, own_ref, a_ref, b_ref, c_ref, out_ref):
    grads = own_ref[...] + a_ref[...].astype(f32) + b_ref[...].astype(f32) + c_ref[...].astype(f32)
    unit, scale = normalize_rows(rows_ref[...])
    out_ref[...] = normalize_back(unit, scale, grads)


def turn(values, axis, step):
    return lax.ppermute(values, axis, [(i, (i + step) % 4) for i in range(4)])


def flip(values, axis):
    return lax.ppermute(values, axis, [(0, 1), (1, 0)])


def over_token_groups(values, beside=()):
    pairs = [(i, i ^ 1) for i in range(4)]
    both = [(z * 2 + c, (z ^ 1) * 2 + (1 - c)) for z in range(4) for c in range(2)]
    terms = flip(values, "c"), lax.ppermute(values, "z", pairs), lax.ppermute(values, ("z", "c"), both)
    core, other, diagonal, *beside = lax.optimization_barrier((*terms, *beside))
    near = (values + core) + (other + diagonal)
    return (near, lax.ppermute(near, "z", [(i, 3 - i) for i in range(4)])), beside


def exchange(blocks):
    return lax.all_to_all(blocks, SAME_TOKENS, 0, 0, tiled=True)


def local(student_patches, teacher_patches, mask_positions, token_weight, student_weight, teacher_weight):
    z, c, y, x = (lax.axis_index(name) for name in ("z", "c", "y", "x"))
    place = jnp.stack([z, c, y, x]).astype(jnp.int32)
    matrix = K * T * 2
    product = 2 * K * T * D
    shape = jax.ShapeDtypeStruct
    row, rows = shape((PACKED, LANES), f32), shape((K // LANES, LANES), f32)
    resident = pltpu.VMEM((K, T), bf16)

    DMA = pltpu.SemaphoreType.DMA
    unit_rows, student_rows = call(
        rows_kernel, [shape((144, D), bf16), shape((64, D), f32)],
        teacher_patches, student_patches, mask_positions, token_weight, far=(0, 1, 2, 3),
        scratch=[
            pltpu.VMEM((2, 256, D), bf16), pltpu.VMEM((2, 256, D), bf16),
            pltpu.VMEM((2, 32), jnp.int32), pltpu.VMEM((2, 32), bf16), DMA((4,)),
        ],
        name="rows",
    )
    unit_rows, place = lax.optimization_barrier((unit_rows, place))
    parts = [unit_rows] + [turn(unit_rows, "y", i) for i in (1, 2, 3)]
    protos = pltpu.VMEM((K, D), bf16)
    loading = dict(far=(0,), scratch=[protos, DMA((K // BLOCK,))])
    (teacher_protos,) = call(protos_kernel, [protos], teacher_weight, name="teacher_protos", moved=2 * K * D, **loading)
    *parts, teacher_protos = lax.optimization_barrier((*parts, teacher_protos))
    column = jnp.concatenate(parts, axis=0)
    halves = jnp.concatenate(parts[0:2], axis=0), jnp.concatenate(parts[2:4], axis=0)
    gathered = [column, turn(column, "x", 1), *(turn(half, "x", 2) for half in halves), turn(column, "x", 3)]
    student_protos, protos_t = call(
        protos_t_kernel, [shape((K, D), bf16), shape((D, K), bf16)], student_weight,
        name="student_protos", moved=2 * K * D, **loading,
    )
    *gathered, student_protos = lax.optimization_barrier((*gathered, student_protos))
    teacher_exp, mass = call(
        teacher_kernel, [resident, rows], place, *gathered, teacher_protos,
        scratch=[pltpu.VMEM((T, D), bf16)], limit=16, name="teacher_exp",
    )
    place, mass = lax.optimization_barrier((place, mass))
    part, student_all, rows_t, weight, early = call(
        student_kernel,
        [shape((8, T), f32), shape((T, D), bf16), shape((D, T), bf16), row, shape((D, T), f32)],
        place, *gathered, student_protos, protos_t,
        scratch=[pltpu.VMEM((GROUPS, 16, LANES), f32)],
        limit=16, name="student_unit_grads", flops=product, moved=matrix // 2, exps=K * T // 2,
    )
    masses, (part, early) = over_token_groups(mass, (part, early))
    total, student_part = call(
        student_rest_kernel, [row, shape((D, T), f32)], student_all, student_protos, protos_t, part, early,
        limit=16, name="student_unit_rest", flops=product, moved=matrix // 2, exps=K * T // 2,
    )
    (copies,) = call(
        first_token_mass_kernel, [shape((GROUPS, PACKED, LANES), f32)], *masses, teacher_exp,
        name="token_mass", moved=matrix // 2,
    )
    copies, total, student_part = lax.optimization_barrier((copies, total, student_part))
    parts = exchange(copies)
    (mass,) = call(
        first_proto_mass_kernel, [rows], parts, teacher_exp, name="proto_mass", moved=matrix // 2
    )
    masses, _ = over_token_groups(mass)
    (copies,) = call(
        token_mass_kernel, [shape((GROUPS, 2 * PACKED, LANES), f32)], *masses, teacher_exp, total,
        name="token_mass", moved=matrix // 2,
    )
    parts = exchange(copies)
    mass, total = call(
        proto_mass_kernel, [rows, row], parts, teacher_exp, name="proto_mass", moved=matrix // 2
    )
    half = [student_protos, student_all, rows_t, total, weight]
    cost = dict(limit=16, flops=product, moved=matrix // 2, exps=K * T // 2)
    (student_proto,) = call(student_proto_kernel, [shape((K, D), bf16)], *half, name="student_proto_grads", **cost)
    masses, (student_proto,) = over_token_groups(mass, (student_proto,))
    (student_proto,) = call(
        student_proto_rest_kernel, [shape((K, D), bf16)], *half, student_proto,
        aliases={5: 0}, name="student_proto_rest", **cost,
    )
    copies, proto_scale, teacher_part = call(
        last_token_mass_kernel,
        [shape((GROUPS, 2 * PACKED, LANES), f32), rows, shape((D, T), f32)],
        *masses, teacher_exp, protos_t, rows_t,
        scratch=[pltpu.VMEM((D + 16, K), bf16)], limit=12, name="last_token_mass", flops=product, moved=matrix,
    )
    copies, student_proto = lax.optimization_barrier((copies, student_proto))
    parts = exchange(copies)
    loss, teacher_scale, own, one, two, three = call(
        combine_kernel,
        [shape((8, LANES), f32), row, shape((256, D), f32)] + [shape((256, D), bf16)] * 3,
        place, parts, total, weight, student_part, teacher_part,
        scratch=[pltpu.VMEM((16, T), f32)], name="combine",
    )
    one, two, three = turn(one, "y", 1), turn(two, "y", 2), turn(three, "y", 3)

    def proto_grads(name, chunks, outs):
        return call(
            lambda *refs: proto_kernel(chunks, *refs), outs,
            place, loss, teacher_scale, proto_scale, rows_t, teacher_exp, student_proto,
            name=name,
        )

    keep = shape((1024, D), f32)
    (far,) = proto_grads("proto_grads_far_send", [(2, True)], [shape((1040, D), bf16)])
    from_far = flip(far, "c")
    teacher_scale, far = lax.optimization_barrier((teacher_scale, far))
    (far_keep,) = proto_grads("proto_grads_far_keep", [(2, False)], [keep])
    piece, side = shape((528, D), bf16), shape((1040, D), bf16)
    up, down, loss_here = call(
        first_fold_kernel, [piece, piece, shape((8, LANES), f32)], far_keep, from_far, loss, name="first_fold",
    )
    up_there, down_there = turn(up, "z", 1), turn(down, "z", 3)
    teacher_scale, loss_here = lax.optimization_barrier((teacher_scale, loss_here))
    (others,) = proto_grads("proto_grads_send", [(1, True), (3, True), (0, True)], [shape((3072, D), bf16)])
    others, teacher_scale, up_there, down_there, one, two, three = lax.optimization_barrier(
        (others, teacher_scale, up_there, down_there, one, two, three)
    )
    from_others = flip(others, "c")
    (others_keep,) = proto_grads("proto_grads_keep", [(1, False), (3, False), (0, False)], [shape((3072, D), f32)])
    own, others_keep = lax.optimization_barrier((own, others_keep))
    own, one, two, three = call(
        fold_rows_kernel, [shape((64, D), f32)] + [shape((64, D), bf16)] * 3,
        place, own, one, two, three, name="fold_rows",
    )
    first, second = call(
        second_fold_kernel, [side, side], others_keep, from_others, up_there, down_there, name="second_fold",
    )
    own, first = lax.optimization_barrier((own, first))
    one, two, three = turn(one, "x", 1), turn(two, "x", 2), turn(three, "x", 3)
    from_last, from_next = turn(first, "z", 1), turn(second, "z", 3)
    unit, scale, base = call(
        own_kernel, [keep, shape((1024, LANES), f32), keep], place, student_weight, others_keep, from_others, far=(1,),
        scratch=[pltpu.VMEM((1024, D), bf16), DMA], name="own",
    )
    (feature_grads,) = call(
        feature_grads_kernel, [shape((64, D), f32)], student_rows, own, one, two, three, name="feature_grads",
    )
    weight_grads, loss = call(
        weight_grads_kernel, [keep, shape((1, 1), f32)],
        unit, scale, base, loss_here, up_there, down_there, from_last, from_next, name="weight_grads",
    )
    return loss.reshape(()), feature_grads.reshape(2, 32, D), weight_grads


def solution(mesh):
    fine = Mesh(mesh.devices.reshape(4, 2, 4, 4), ("z", "c", "y", "x"))
    every, proto = ("z", "c", "y", "x"), ("y", "x")
    return jax.shard_map(
        local,
        mesh=fine,
        in_specs=(
            P(every, None, None),
            P(every, None, None),
            P(every, None),
            P(every, None),
            P(proto, None),
            P(proto, None),
        ),
        out_specs=(P(), P(every, None, None), P(("y", "x", "z", "c"), None)),
        check_vma=False,
    )
```

```python
import jax
import jax.numpy as jnp
from jax import lax
from jax.experimental import pallas as pl
from jax.experimental.pallas import tpu as pltpu
from jax.sharding import Mesh, PartitionSpec as P

teacher_temp = 0.07
student_temp = 0.1
epsilon = 1e-06
LOG2E = 1.4426950408889634
SWEEPS = 3
TOKENS = 8192
T, K, D = 1024, 8192, 256
BLOCK = 512
HALF = 8
LANES = 128
f32, bf16 = jnp.float32, jnp.bfloat16
GROUPS = 16
PACKED = T // LANES
SAME_TOKENS = ("y", "x")
VMEM = pl.BlockSpec(memory_space=pltpu.VMEM)
SMEM = pl.BlockSpec(memory_space=pltpu.SMEM)


def nt(left, right):
    return lax.dot_general(left, right, (((1,), (1,)), ((), ())), preferred_element_type=f32)


def nn(left, right):
    return lax.dot_general(left, right, (((1,), (0,)), ((), ())), preferred_element_type=f32)


def normalize_rows(values):
    scale = lax.rsqrt(jnp.sum(values * values, axis=-1, keepdims=True) + epsilon)
    return values * scale, scale


def three_rows(row):
    high = row.astype(bf16).astype(f32)
    rest = row - high
    middle = rest.astype(bf16).astype(f32)
    low = rest - middle
    index = lax.broadcasted_iota(jnp.int32, (16, row.shape[1]), 0)
    picked = jnp.where(index == 0, high, jnp.where(index == 1, middle, jnp.where(index == 2, low, 0.0)))
    return picked.astype(bf16)


def as_row(packed):
    return jnp.concatenate([packed[j : j + 1, :] for j in range(packed.shape[0])], axis=1)


def store_packed(ref, start, row):
    for j in range(row.shape[1] // LANES):
        ref[start + j : start + j + 1, :] = row[:, j * LANES : (j + 1) * LANES]


def call(kernel, outs, *args, far=(), aliases=None, scratch=(), limit=11, name=None, flops=0, moved=0, exps=0):
    specs = [SMEM if arg.dtype == jnp.int32 and arg.ndim == 1 else VMEM for arg in args]
    args = list(args)
    for i in far:
        specs[i] = pl.BlockSpec(memory_space=pl.ANY)
        args[i] = pltpu.with_memory_space_constraint(args[i], pltpu.HBM)
    return pl.pallas_call(
        kernel,
        out_shape=outs,
        in_specs=specs,
        out_specs=[VMEM] * len(outs),
        scratch_shapes=list(scratch),
        input_output_aliases=aliases or {},
        compiler_params=pltpu.CompilerParams(vmem_limit_bytes=limit << 20),
        cost_estimate=pl.CostEstimate(flops=flops, bytes_accessed=moved, transcendentals=exps),
        name=name,
    )(*args)


def lane_sums(values):
    part = values[:, 0:LANES]
    for j in range(1, values.shape[1] // LANES):
        part = part + values[:, j * LANES : (j + 1) * LANES]
    return jnp.sum(jnp.transpose(part), axis=0, keepdims=True)


def pick_rows(patches_ref, positions_ref, image):
    patch = lax.broadcasted_iota(jnp.int32, (256, 32), 0)
    chosen = (patch == positions_ref[image : image + 1, :]).astype(f32).astype(bf16)
    return lax.dot_general(chosen, patches_ref[image], (((0,), (0,)), ((), ())), preferred_element_type=f32)


def rows_kernel(
    far_teacher_ref, far_student_ref, far_positions_ref, far_weight_ref, unit_ref, rows_ref,
    teacher_ref, student_ref, positions_ref, weight_ref, arrived
):
    pairs = (
        (far_positions_ref, positions_ref), (far_teacher_ref, teacher_ref),
        (far_student_ref, student_ref), (far_weight_ref, weight_ref),
    )
    reads = [pltpu.make_async_copy(far, near, arrived.at[i]) for i, (far, near) in enumerate(pairs)]
    for read in reads:
        read.start()
    reads[0].wait()
    reads[1].wait()
    for image in range(2):
        here = slice(image * 32, (image + 1) * 32)
        unit_ref[here, :] = normalize_rows(pick_rows(teacher_ref, positions_ref, image))[0].astype(bf16)
    reads[2].wait()
    for image in range(2):
        here = slice(image * 32, (image + 1) * 32)
        rows = pick_rows(student_ref, positions_ref, image)
        rows_ref[here, :] = rows
        unit_ref[64 + image * 32 : 96 + image * 32, :] = normalize_rows(rows)[0].astype(bf16)
    reads[3].wait()
    row = lax.broadcasted_iota(jnp.int32, (16, 32), 0)
    weight = weight_ref[...].astype(f32)
    weight = jnp.where(row == 0, weight[0:1], jnp.where(row == 1, weight[1:2], 0.0)).astype(bf16)
    same = lax.broadcasted_iota(jnp.int32, (32, D), 0) == lax.broadcasted_iota(jnp.int32, (32, D), 1)
    unit_ref[128:144, :] = nn(weight, same.astype(f32).astype(bf16)).astype(bf16)


def source(place_ref, y_step, x_step):
    return lax.rem(place_ref[2] + 4 - y_step, 4) * 4 + lax.rem(place_ref[3] + 4 - x_step, 4)


def fetch(far_ref, near_ref, arrived):
    reads = [
        pltpu.make_async_copy(
            far_ref.at[pl.ds(b * BLOCK, BLOCK), :], near_ref.at[pl.ds(b * BLOCK, BLOCK), :], arrived.at[b]
        )
        for b in range(K // BLOCK)
    ]
    for read in reads:
        read.start()
    return reads


def protos_kernel(far_weight_ref, out_ref, weight_ref, arrived):
    for b, read in enumerate(fetch(far_weight_ref, weight_ref, arrived)):
        here = slice(b * BLOCK, (b + 1) * BLOCK)
        read.wait()
        out_ref[here, :] = normalize_rows(weight_ref[here, :].astype(f32))[0].astype(bf16)


def protos_t_kernel(far_weight_ref, out_ref, out_t_ref, weight_ref, arrived):
    for b, read in enumerate(fetch(far_weight_ref, weight_ref, arrived)):
        here = slice(b * BLOCK, (b + 1) * BLOCK)
        read.wait()
        protos = normalize_rows(weight_ref[here, :].astype(f32))[0].astype(bf16)
        out_ref[here, :] = protos
        out_t_ref[:, here] = jnp.transpose(protos.astype(f32)).astype(bf16)


def gathered_blocks(place_ref, a_ref, b_ref, c_ref, c2_ref, d_ref):
    for x_step, refs in enumerate(((a_ref,), (b_ref,), (c_ref, c2_ref), (d_ref,))):
        for y_step in range(4):
            ref, at = refs[y_step * len(refs) // 4], y_step % (4 // len(refs)) * 144
            yield source(place_ref, y_step, x_step), ref, at


def teacher_kernel(place_ref, a_ref, b_ref, c_ref, c2_ref, d_ref, protos_ref, exp_ref, mass_ref, rows_ref):
    for place, ref, at in gathered_blocks(place_ref, a_ref, b_ref, c_ref, c2_ref, d_ref):
        rows_ref[pl.ds(pl.multiple_of(place * 64, 64), 64), :] = ref[at : at + 64, :]
    rows = rows_ref[...]
    for b in range(K // BLOCK):
        here = slice(b * BLOCK, (b + 1) * BLOCK)
        values = jnp.exp2(nt(protos_ref[here, :], rows) * (LOG2E / teacher_temp))
        exp_ref[here, :] = values.astype(bf16)
        store_packed(mass_ref, b * BLOCK // LANES, lane_sums(values))


def student_kernel(
    place_ref, a_ref, b_ref, c_ref, c2_ref, d_ref, protos_ref, protos_t_ref,
    total_ref, rows_ref, rows_t_ref, token_weight_ref, grads_ref, extra_ref
):
    for place, ref, at in gathered_blocks(place_ref, a_ref, b_ref, c_ref, c2_ref, d_ref):
        rows_ref[pl.ds(pl.multiple_of(place * 64, 64), 64), :] = ref[at + 64 : at + 128, :]
        extra_ref[pl.ds(place, 1)] = ref[at + 128 : at + 144, 0:LANES].astype(f32)[None]
    rows = rows_ref[...]
    rows_t_ref[...] = jnp.transpose(rows.astype(f32)).astype(bf16)
    for j in range(PACKED):
        row = jnp.zeros((1, LANES), f32)
        for piece in range(4):
            row = row + pltpu.roll(extra_ref[2 * j + piece // 2], piece * 32, 1)[piece % 2 : piece % 2 + 1]
        token_weight_ref[j : j + 1, :] = row
    grads_ref[...] = jnp.zeros_like(grads_ref)
    total = jnp.zeros((8, T), f32)
    total_ref[...] = student_blocks(0, HALF, rows, protos_ref, protos_t_ref, grads_ref, total)


def student_blocks(first, last, rows, protos_ref, protos_t_ref, grads_ref, total):
    def step(b, total):
        here = pl.ds(pl.multiple_of(b * BLOCK, BLOCK), BLOCK)
        values = jnp.exp2(nt(protos_ref[here, :], rows) * (LOG2E / student_temp))
        grads_ref[...] += nn(protos_t_ref[:, here], values.astype(bf16))
        return total + jnp.sum(values.reshape(BLOCK // 8, 8, T), axis=0)

    return lax.fori_loop(first, last, step, total, unroll=4)


def student_rest_kernel(rows_ref, protos_ref, protos_t_ref, part_ref, early_ref, total_ref, grads_ref):
    grads_ref[...] = early_ref[...]
    total = student_blocks(HALF, K // BLOCK, rows_ref[...], protos_ref, protos_t_ref, grads_ref, part_ref[...])
    store_packed(total_ref, 0, jnp.sum(total, axis=0, keepdims=True))


def student_proto_rest_kernel(protos_ref, rows_ref, rows_t_ref, total_ref, weight_ref, held_ref, out_ref):
    student_proto_blocks(HALF, K // BLOCK, protos_ref, rows_ref, rows_t_ref, total_ref, weight_ref, out_ref)


def student_proto_kernel(*refs):
    student_proto_blocks(0, HALF, *refs)


def student_proto_blocks(first, last, protos_ref, rows_ref, rows_t_ref, total_ref, weight_ref, out_ref):
    rows = rows_ref[...]
    scale = as_row(weight_ref[...] / (student_temp * total_ref[...]))
    right = (rows_t_ref[...].astype(f32) * scale).astype(bf16)

    def step(b, carry):
        here = pl.ds(pl.multiple_of(b * BLOCK, BLOCK), BLOCK)
        values = jnp.exp2(nt(protos_ref[here, :], rows) * (LOG2E / student_temp))
        out_ref[here, :] = nt(values.astype(bf16), right).astype(bf16)
        return carry

    lax.fori_loop(first, last, step, 0, unroll=8)


def store_copies(ref, start, row):
    for j in range(row.shape[1] // LANES):
        piece = row[:, j * LANES : (j + 1) * LANES]
        for copy in range(GROUPS):
            ref[copy, start + j : start + j + 1, :] = piece


def token_mass(packed, exp_ref, mass_ref):
    scale = three_rows(as_row(packed))
    total = jnp.zeros((16, T), f32)
    for b in range(K // BLOCK):
        here = slice(b * BLOCK, (b + 1) * BLOCK)
        total = total + nn(scale[:, here], exp_ref[here, :])
    store_copies(mass_ref, 0, jnp.sum(total, axis=0, keepdims=True))


def first_token_mass_kernel(near_ref, far_ref, exp_ref, mass_ref):
    token_mass(1.0 / (near_ref[...] + far_ref[...]), exp_ref, mass_ref)


def token_mass_kernel(near_ref, far_ref, exp_ref, student_ref, mass_ref):
    token_mass(1.0 / (near_ref[...] + far_ref[...]), exp_ref, mass_ref)
    student = student_ref[...]
    for copy in range(GROUPS):
        mass_ref[copy, PACKED : 2 * PACKED, :] = student


def last_token_mass_kernel(
    near_ref, far_ref, exp_ref, protos_t_ref, rows_t_ref, mass_ref, scale_ref, grads_ref, left_ref
):
    packed = 1.0 / (near_ref[...] + far_ref[...])
    scale_ref[...] = packed
    scale = as_row(packed)
    left_ref[D : D + 16, :] = three_rows(scale)
    left_ref[0:D, :] = (protos_t_ref[...].astype(f32) * scale).astype(bf16)
    for j in range(T // BLOCK):
        here = slice(j * BLOCK, (j + 1) * BLOCK)
        both = nn(left_ref[...], exp_ref[:, here])
        grads = both[0:D]
        grads_ref[:, here] = grads
        store_copies(mass_ref, j * BLOCK // LANES, jnp.sum(both[D:], axis=0, keepdims=True))
        cross = jnp.sum(grads * rows_t_ref[:, here].astype(f32), axis=0, keepdims=True)
        store_copies(mass_ref, (T + j * BLOCK) // LANES, cross)


def column_mass(scale, exp_ref, mass_ref):
    split = three_rows(scale)
    for b in range(K // 1024):
        start = b * 1024 + 640
        row = jnp.sum(nt(split, exp_ref[start : start + 384, :]), axis=0, keepdims=True)
        store_packed(mass_ref, start // LANES, row)
        start = b * 1024
        part = jnp.zeros((640, LANES), f32)
        for j in range(T // LANES):
            lanes = slice(j * LANES, (j + 1) * LANES)
            part = part + exp_ref[start : start + 640, lanes].astype(f32) * scale[:, lanes]
        store_packed(mass_ref, start // LANES, jnp.sum(jnp.transpose(part), axis=0, keepdims=True))


def first_proto_mass_kernel(parts_ref, exp_ref, mass_ref):
    column_mass(1.0 / as_row(jnp.sum(parts_ref[...], axis=0)), exp_ref, mass_ref)


def proto_mass_kernel(parts_ref, exp_ref, mass_ref, total_ref):
    parts = jnp.sum(parts_ref[...], axis=0)
    total_ref[...] = parts[PACKED:]
    column_mass(1.0 / as_row(parts[0:PACKED]), exp_ref, mass_ref)


def combine_kernel(
    place_ref, parts_ref, total_ref, weight_ref, student_ref, teacher_ref,
    loss_ref, scale_ref, keep_ref, one_ref, two_ref, three_ref, rows_ref
):
    parts = jnp.sum(parts_ref[...], axis=0)
    token_scale = 1.0 / parts[0:PACKED]
    total, weight = total_ref[...], weight_ref[...]
    cross = jnp.log(total) - token_scale * parts[PACKED:] / student_temp
    loss_ref[...] = jnp.full((8, LANES), jnp.sum(weight * cross) / TOKENS, f32)
    teacher_scale = weight * token_scale / student_temp
    scale_ref[...] = teacher_scale
    rows_ref[0:1, :] = as_row(weight / (student_temp * total))
    rows_ref[8:9, :] = as_row(teacher_scale)
    for step, ref in enumerate((keep_ref, one_ref, two_ref, three_ref)):
        block = lax.rem(place_ref[2] + step, 4)
        here = pl.ds(pl.multiple_of(block * 256, 256), 256)
        grads = student_ref[:, here] * rows_ref[0:1, here] - teacher_ref[:, here] * rows_ref[8:9, here]
        ref[...] = jnp.transpose(grads).astype(ref.dtype)


def fold_rows_kernel(place_ref, own_ref, a_ref, b_ref, c_ref, keep_ref, one_ref, two_ref, three_ref):
    for step, ref in enumerate((keep_ref, one_ref, two_ref, three_ref)):
        block = lax.rem(place_ref[3] + step, 4)
        here = pl.ds(pl.multiple_of(block * 64, 64), 64)
        total = own_ref[here, :] + a_ref[here, :].astype(f32) + b_ref[here, :].astype(f32)
        ref[...] = (total + c_ref[here, :].astype(f32)).astype(ref.dtype)


def proto_kernel(chunks, place_ref, loss_ref, teacher_scale_ref, scale_ref, rows_t_ref, exp_ref, student_ref, *outs):
    right = (rows_t_ref[...].astype(f32) * as_row(teacher_scale_ref[...])).astype(bf16)
    places = [(ref, i * 1024) for ref in outs for i in range(ref.shape[0] // 1024)]
    for (z_step, core_flip), (ref, first) in zip(chunks, places):
        z = lax.rem(place_ref[0] + z_step, 4)
        core = 1 - place_ref[1] if core_flip else place_ref[1]
        chunk = z * 2 + core
        if ref.shape[0] == 1040:
            ref[1024:1040, :] = loss_rows(loss_ref[0:1, :])
        for b in range(2):
            start = pl.multiple_of(chunk * 1024 + b * 512, 512)
            product = nt(exp_ref[pl.ds(start, 512), :], right)
            student = student_ref[pl.ds(start, 512), :].astype(f32)
            for j in range(4):
                row = scale_ref[pl.ds(chunk * 8 + b * 4 + j, 1), :]
                column = jnp.transpose(jnp.broadcast_to(row, (LANES, LANES)))
                column = jnp.concatenate([column, column], axis=1)
                here = slice(j * LANES, (j + 1) * LANES)
                value = student[here] - product[here] * column
                to = first + b * 512 + j * LANES
                ref[to : to + LANES, :] = value.astype(ref.dtype)


def loss_rows(row):
    return three_rows(jnp.concatenate([row, row], axis=1))


def loss_of(rows):
    return jnp.sum(rows.astype(f32), axis=0, keepdims=True)[:, 0:LANES]


def first_fold_kernel(own_ref, core_ref, loss_ref, up_ref, down_ref, loss_out_ref):
    loss = loss_ref[0:1, :] + loss_of(core_ref[1024:1040, :])
    loss_out_ref[...] = jnp.broadcast_to(loss, (8, LANES))
    for i, ref in enumerate((up_ref, down_ref)):
        here = slice(i * 512, (i + 1) * 512)
        ref[0:512, :] = (own_ref[here, :] + core_ref[here, :].astype(f32)).astype(bf16)
        ref[512:528, :] = loss_rows(loss)


def second_fold_kernel(own_ref, core_ref, up_ref, down_ref, next_ref, last_ref):
    for i in range(4):
        here = slice(i * 512, (i + 1) * 512)
        value = own_ref[here, :] + core_ref[here, :].astype(f32)
        if i in (0, 3):
            value = value + (up_ref if i == 0 else down_ref)[0:512, :].astype(f32)
        to = i % 2 * 512
        (next_ref if i < 2 else last_ref)[to : to + 512, :] = value.astype(bf16)
    next_ref[1024:1040, :] = up_ref[512:528, :]
    last_ref[1024:1040, :] = up_ref[512:528, :]


def normalize_back(unit, scale, grad):
    return scale * (grad - unit * jnp.sum(unit * grad, axis=-1, keepdims=True))


def own_kernel(place_ref, far_weight_ref, own_ref, core_ref, unit_ref, scale_ref, base_ref, weight_ref, arrived):
    start = pl.multiple_of((place_ref[0] * 2 + place_ref[1]) * 1024, 1024)
    read = pltpu.make_async_copy(far_weight_ref.at[pl.ds(start, 1024), :], weight_ref, arrived)
    read.start()
    base_ref[...] = own_ref[2048:3072, :] + core_ref[2048:3072, :].astype(f32)
    read.wait()
    unit, scale = normalize_rows(weight_ref[...].astype(f32))
    unit_ref[...] = unit
    scale_ref[...] = jnp.broadcast_to(scale, (1024, LANES))


def weight_grads_kernel(
    unit_ref, scale_ref, base_ref, loss_ref, up_ref, down_ref, last_ref, next_ref, out_ref, loss_out_ref
):
    far = loss_ref[0:1, :] + loss_of(last_ref[1024:1040, :])
    loss = far + (loss_of(up_ref[512:528, :]) + loss_of(down_ref[512:528, :]))
    loss_out_ref[...] = loss[:, 0:1]
    grads = base_ref[...] + (last_ref[0:1024, :].astype(f32) + next_ref[0:1024, :].astype(f32))
    out_ref[...] = normalize_back(unit_ref[...], scale_ref[:, 0:1], grads)


def feature_grads_kernel(rows_ref, own_ref, a_ref, b_ref, c_ref, out_ref):
    grads = own_ref[...] + a_ref[...].astype(f32) + b_ref[...].astype(f32) + c_ref[...].astype(f32)
    unit, scale = normalize_rows(rows_ref[...])
    out_ref[...] = normalize_back(unit, scale, grads)


def turn(values, axis, step):
    return lax.ppermute(values, axis, [(i, (i + step) % 4) for i in range(4)])


def flip(values, axis):
    return lax.ppermute(values, axis, [(0, 1), (1, 0)])


def over_token_groups(values, beside=()):
    pairs = [(i, i ^ 1) for i in range(4)]
    both = [(z * 2 + c, (z ^ 1) * 2 + (1 - c)) for z in range(4) for c in range(2)]
    terms = flip(values, "c"), lax.ppermute(values, "z", pairs), lax.ppermute(values, ("z", "c"), both)
    core, other, diagonal, *beside = lax.optimization_barrier((*terms, *beside))
    near = (values + core) + (other + diagonal)
    return (near, lax.ppermute(near, "z", [(i, 3 - i) for i in range(4)])), beside


def exchange(blocks):
    return lax.all_to_all(blocks, SAME_TOKENS, 0, 0, tiled=True)


def local(student_patches, teacher_patches, mask_positions, token_weight, student_weight, teacher_weight):
    z, c, y, x = (lax.axis_index(name) for name in ("z", "c", "y", "x"))
    place = jnp.stack([z, c, y, x]).astype(jnp.int32)
    matrix = K * T * 2
    product = 2 * K * T * D
    shape = jax.ShapeDtypeStruct
    row, rows = shape((PACKED, LANES), f32), shape((K // LANES, LANES), f32)
    resident = pltpu.VMEM((K, T), bf16)

    DMA = pltpu.SemaphoreType.DMA
    unit_rows, student_rows = call(
        rows_kernel, [shape((144, D), bf16), shape((64, D), f32)],
        teacher_patches, student_patches, mask_positions, token_weight, far=(0, 1, 2, 3),
        scratch=[
            pltpu.VMEM((2, 256, D), bf16), pltpu.VMEM((2, 256, D), bf16),
            pltpu.VMEM((2, 32), jnp.int32), pltpu.VMEM((2, 32), bf16), DMA((4,)),
        ],
        name="rows",
    )
    unit_rows, place = lax.optimization_barrier((unit_rows, place))
    parts = [unit_rows] + [turn(unit_rows, "y", i) for i in (1, 2, 3)]
    protos = pltpu.VMEM((K, D), bf16)
    loading = dict(far=(0,), scratch=[protos, DMA((K // BLOCK,))])
    (teacher_protos,) = call(protos_kernel, [protos], teacher_weight, name="teacher_protos", moved=2 * K * D, **loading)
    *parts, teacher_protos = lax.optimization_barrier((*parts, teacher_protos))
    column = jnp.concatenate(parts, axis=0)
    halves = jnp.concatenate(parts[0:2], axis=0), jnp.concatenate(parts[2:4], axis=0)
    gathered = [column, turn(column, "x", 1), *(turn(half, "x", 2) for half in halves), turn(column, "x", 3)]
    student_protos, protos_t = call(
        protos_t_kernel, [shape((K, D), bf16), shape((D, K), bf16)], student_weight,
        name="student_protos", moved=2 * K * D, **loading,
    )
    *gathered, student_protos = lax.optimization_barrier((*gathered, student_protos))
    teacher_exp, mass = call(
        teacher_kernel, [resident, rows], place, *gathered, teacher_protos,
        scratch=[pltpu.VMEM((T, D), bf16)], limit=16, name="teacher_exp",
    )
    place, mass = lax.optimization_barrier((place, mass))
    part, student_all, rows_t, weight, early = call(
        student_kernel,
        [shape((8, T), f32), shape((T, D), bf16), shape((D, T), bf16), row, shape((D, T), f32)],
        place, *gathered, student_protos, protos_t,
        scratch=[pltpu.VMEM((GROUPS, 16, LANES), f32)],
        limit=16, name="student_unit_grads", flops=product, moved=matrix // 2, exps=K * T // 2,
    )
    masses, (part, early) = over_token_groups(mass, (part, early))
    total, student_part = call(
        student_rest_kernel, [row, shape((D, T), f32)], student_all, student_protos, protos_t, part, early,
        limit=16, name="student_unit_rest", flops=product, moved=matrix // 2, exps=K * T // 2,
    )
    (copies,) = call(
        first_token_mass_kernel, [shape((GROUPS, PACKED, LANES), f32)], *masses, teacher_exp,
        name="token_mass", moved=matrix // 2,
    )
    copies, total, student_part = lax.optimization_barrier((copies, total, student_part))
    parts = exchange(copies)
    (mass,) = call(
        first_proto_mass_kernel, [rows], parts, teacher_exp, name="proto_mass", moved=matrix // 2
    )
    masses, _ = over_token_groups(mass)
    (copies,) = call(
        token_mass_kernel, [shape((GROUPS, 2 * PACKED, LANES), f32)], *masses, teacher_exp, total,
        name="token_mass", moved=matrix // 2,
    )
    parts = exchange(copies)
    mass, total = call(
        proto_mass_kernel, [rows, row], parts, teacher_exp, name="proto_mass", moved=matrix // 2
    )
    half = [student_protos, student_all, rows_t, total, weight]
    cost = dict(limit=16, flops=product, moved=matrix // 2, exps=K * T // 2)
    (student_proto,) = call(student_proto_kernel, [shape((K, D), bf16)], *half, name="student_proto_grads", **cost)
    masses, (student_proto,) = over_token_groups(mass, (student_proto,))
    (student_proto,) = call(
        student_proto_rest_kernel, [shape((K, D), bf16)], *half, student_proto,
        aliases={5: 0}, name="student_proto_rest", **cost,
    )
    copies, proto_scale, teacher_part = call(
        last_token_mass_kernel,
        [shape((GROUPS, 2 * PACKED, LANES), f32), rows, shape((D, T), f32)],
        *masses, teacher_exp, protos_t, rows_t,
        scratch=[pltpu.VMEM((D + 16, K), bf16)], limit=12, name="last_token_mass", flops=product, moved=matrix,
    )
    copies, student_proto = lax.optimization_barrier((copies, student_proto))
    parts = exchange(copies)
    loss, teacher_scale, own, one, two, three = call(
        combine_kernel,
        [shape((8, LANES), f32), row, shape((256, D), f32)] + [shape((256, D), bf16)] * 3,
        place, parts, total, weight, student_part, teacher_part,
        scratch=[pltpu.VMEM((16, T), f32)], name="combine",
    )
    one, two, three = turn(one, "y", 1), turn(two, "y", 2), turn(three, "y", 3)

    def proto_grads(name, chunks, outs):
        return call(
            lambda *refs: proto_kernel(chunks, *refs), outs,
            place, loss, teacher_scale, proto_scale, rows_t, teacher_exp, student_proto,
            name=name,
        )

    keep = shape((1024, D), f32)
    (far,) = proto_grads("proto_grads_far_send", [(2, True)], [shape((1040, D), bf16)])
    from_far = flip(far, "c")
    teacher_scale, far = lax.optimization_barrier((teacher_scale, far))
    (far_keep,) = proto_grads("proto_grads_far_keep", [(2, False)], [keep])
    piece, side = shape((528, D), bf16), shape((1040, D), bf16)
    up, down, loss_here = call(
        first_fold_kernel, [piece, piece, shape((8, LANES), f32)], far_keep, from_far, loss, name="first_fold",
    )
    up_there, down_there = turn(up, "z", 1), turn(down, "z", 3)
    teacher_scale, loss_here = lax.optimization_barrier((teacher_scale, loss_here))
    (others,) = proto_grads("proto_grads_send", [(1, True), (3, True), (0, True)], [shape((3072, D), bf16)])
    others, teacher_scale, up_there, down_there, one, two, three = lax.optimization_barrier(
        (others, teacher_scale, up_there, down_there, one, two, three)
    )
    from_others = flip(others, "c")
    (others_keep,) = proto_grads("proto_grads_keep", [(1, False), (3, False), (0, False)], [shape((3072, D), f32)])
    own, others_keep = lax.optimization_barrier((own, others_keep))
    own, one, two, three = call(
        fold_rows_kernel, [shape((64, D), f32)] + [shape((64, D), bf16)] * 3,
        place, own, one, two, three, name="fold_rows",
    )
    first, second = call(
        second_fold_kernel, [side, side], others_keep, from_others, up_there, down_there, name="second_fold",
    )
    own, first = lax.optimization_barrier((own, first))
    one, two, three = turn(one, "x", 1), turn(two, "x", 2), turn(three, "x", 3)
    from_last, from_next = turn(first, "z", 1), turn(second, "z", 3)
    unit, scale, base = call(
        own_kernel, [keep, shape((1024, LANES), f32), keep], place, student_weight, others_keep, from_others, far=(1,),
        scratch=[pltpu.VMEM((1024, D), bf16), DMA], name="own",
    )
    (feature_grads,) = call(
        feature_grads_kernel, [shape((64, D), f32)], student_rows, own, one, two, three, name="feature_grads",
    )
    weight_grads, loss = call(
        weight_grads_kernel, [keep, shape((1, 1), f32)],
        unit, scale, base, loss_here, up_there, down_there, from_last, from_next, name="weight_grads",
    )
    return loss.reshape(()), feature_grads.reshape(2, 32, D), weight_grads


def solution(mesh):
    fine = Mesh(mesh.devices.reshape(4, 2, 4, 4), ("z", "c", "y", "x"))
    every, proto = ("z", "c", "y", "x"), ("y", "x")
    return jax.shard_map(
        local,
        mesh=fine,
        in_specs=(
            P(every, None, None),
            P(every, None, None),
            P(every, None),
            P(every, None),
            P(proto, None),
            P(proto, None),
        ),
        out_specs=(P(), P(every, None, None), P(("y", "x", "z", "c"), None)),
        check_vma=False,
    )
```
